32 devices in a mesh: dp: 4 (over x, core), expert: 2 (over y), seq: 4 (over z).
Axes of the slice: x: 2, y: 2, z: 4, core: 2. Of those that a mesh axis runs over, the one named last changes fastest.
Arguments:
- tokens: bfloat16 [4096, 4096], P(('dp', 'expert', 'seq')), may hold values from -6 to 6
- out_grad: bfloat16 [4096, 4096], P(('dp', 'expert', 'seq')), may hold values from -1.5 to 1.5
- gate_prob: bfloat16 [4096], P(('dp', 'expert', 'seq')), may hold values from 0.099609375 to 1
- expert_ids: int32 [4096, 1], P(('dp', 'expert', 'seq')), may hold values from 0 to 1; in each aligned block of 128 rows (0 to 127, 128 to 255, ...) at most 68 rows name the same one
- w_gate: bfloat16 [2, 4096, 1536], P('expert', None, 'seq'), may hold values from -0.09375 to 0.09375
- w_up: bfloat16 [2, 4096, 1536], P('expert', None, 'seq'), may hold values from -0.09375 to 0.09375
- w_down: bfloat16 [2, 1536, 4096], P('expert', 'seq'), may hold values from -0.15625 to 0.15625
Outputs:
- token_grad: bfloat16 [4096, 4096], P(('dp', 'expert', 'seq'))
- gate_grad: bfloat16 [4096], P(('dp', 'expert', 'seq'))
- gate_w_grad: bfloat16 [2, 4096, 1536], P('expert', 'dp', 'seq')
- up_w_grad: bfloat16 [2, 4096, 1536], P('expert', 'dp', 'seq')
- down_w_grad: bfloat16 [2, 1536, 4096], P('expert', 'seq', 'dp')
The draws below stay inside these ranges and needn't reach their ends.
Inputs may be any that keep to these rules, and one draw needn't show every extreme that they name: `expert_ids`: in the 128 rows of one device no expert is named more than 68 times, a bound that some block reaches.
All inputs are finite; a program needn't handle non-finite values.
Results may differ from the reference program's by a relative error of at most 0.009.
Values may be sent and summed in bfloat16 or wider, within the bound.
No kernel may reach another device: no remote copies, remote signals or barrier semaphores. Data moves between devices by JAX's collectives and lax.ppermute only.
A program may use at most 192 MiB of HBM per device.

```python
import math
import jax
import jax.numpy as jnp
import numpy as np
from jax import lax

D = 4096
H = 1536
TOP = 1
TOK_DEV = 128
EXPERTS = 2
CAP = 68
TOKENS = 4096
N_DP = 4
N_EXPERT = 2
N_SEQ = 4


def steps_of(own_key, extent, shards, low, largest):
    loudness, own = 1.0, jax.random.fold_in(own_key, 6)
    for position, shards_of in shards:
        steps = jnp.exp(jax.random.uniform(jax.random.fold_in(own, position), (shards_of,), jnp.float32, low / len(shards), largest / len(shards)))
        loudness = loudness * jnp.repeat(steps, extent[position] // shards_of).reshape([-1 if axis == position else 1 for axis in range(len(extent))])
    return loudness


def shared_out(key, own, number, rows, amount, top, bound, slope):
    order = jax.random.permutation(key, amount)
    heavy_load, common = portions_of(amount, rows * top, bound, slope, True), portions_of(amount, rows * top, bound, slope, False)
    places = jnp.arange(amount)

    def named(sizes, offset_by):
        used = int((sizes > 0).sum())
        fixed = max(1, used // 4)
        shifted = fixed + (places - fixed + offset_by * (used - fixed)) % max(1, amount - fixed)
        return jnp.zeros((amount,), jnp.int32).at[order[jnp.where(places < fixed, places, shifted)]].set(jnp.asarray(sizes, jnp.int32))

    sizes = jnp.where(number % 4 == 0, named(heavy_load, number // 4), named(common, number - number // 4 - 1))
    mixed = jax.random.permutation(jax.random.fold_in(own, 3), amount)
    source_of, taker = mixed[0:amount // 2 * 2:2], mixed[1:amount // 2 * 2:2]
    slack = jnp.minimum(sizes[source_of] - 1, bound - sizes[taker]) // 2
    slack = jnp.where((source_of == order[0]) | (taker == order[0]) | (sizes[taker] == 0), 0, jnp.maximum(slack, 0))
    shifted = jax.random.randint(jax.random.fold_in(own, 4), (amount // 2,), 0, 1 << 20) % (slack + 1)
    sizes = sizes.at[source_of].add(-shifted).at[taker].add(shifted)
    members = jnp.searchsorted(jnp.cumsum(sizes), jnp.arange(rows * top), side="right").astype(jnp.int32)
    listing = members.reshape(top, rows).T
    listing = listing[jax.random.permutation(jax.random.fold_in(own, 1), rows)]
    offset_by = jax.random.randint(jax.random.fold_in(own, 2), (rows, 1), 0, top)
    return jnp.take_along_axis(listing, (jnp.arange(top)[None, :] + offset_by) % top, axis=1)


def portions_of(amount, total, most, lean, full):
    portions = [(1 << 20) // math.isqrt(rank ** lean) + 1 for rank in range(1, amount + 1)]
    largest = most if full else min(most, max(-(-total // amount), total * portions[0] // sum(portions)))
    least = 1 if total - largest >= amount - 1 else 0
    counts, rest = [largest] + [least] * (amount - 1), total - largest - least * (amount - 1)
    while rest > 0:
        candidates = [i for i in range(1, amount) if counts[i] < largest] or [i for i in range(1, amount) if counts[i] < most]
        mass, remaining = sum([portions[i] for i in candidates]), rest
        for i in candidates:
            extra = min(most - counts[i], max(1, remaining * portions[i] // mass), rest)
            counts[i] = counts[i] + extra
            rest = rest - extra
    return np.array(counts)


def noise(stream_key, extent, deviation, most, pieces=(), dtype=jnp.bfloat16):
    factor_of = steps_of(stream_key, extent, pieces, -0.22, 0.18) if pieces else 1.0
    result = jax.random.normal(stream_key, extent, jnp.float32) * deviation * factor_of
    return jnp.minimum(jnp.maximum(result, -most), most).astype(dtype)


def setup_inputs(seed: int = 0) -> dict:
    seeds = jax.random.split(jax.random.key(seed), 8)
    tokens = noise(seeds[0], (TOKENS, D), 1.0, 6.0, ((0, 32),))
    out_grad = noise(seeds[1], (TOKENS, D), 0.25, 1.5, ((0, 32),))
    gate_prob = jnp.clip(jnp.exp(math.log(1.0) - 2.306499 * jax.random.uniform(seeds[2], (TOKENS,), jnp.float32) ** steps_of(seeds[2], (TOKENS,), ((0, 32),), -0.2, 0.2)), 0.099609375, 1.0).astype(jnp.bfloat16)
    expert_ids_keys = jax.random.split(jax.random.fold_in(seeds[3], 1), TOKENS // TOK_DEV)
    expert_ids_turns = jax.random.permutation(jax.random.fold_in(seeds[3], 3), TOKENS // TOK_DEV)
    expert_ids = jax.vmap(lambda own, number: shared_out(jax.random.fold_in(seeds[3], 2), own, number, TOK_DEV, EXPERTS, TOP, CAP, 1))(expert_ids_keys, expert_ids_turns).reshape((TOKENS, TOP))
    w_gate = noise(seeds[4], (EXPERTS, D, H), D ** -0.5, 0.09375, ((0, 2), (2, 4)))
    w_up = noise(seeds[5], (EXPERTS, D, H), D ** -0.5, 0.09375, ((0, 2), (2, 4)))
    w_down = noise(seeds[6], (EXPERTS, H, D), H ** -0.5, 0.15625, ((0, 2), (1, 4)))
    return {"tokens": tokens, "out_grad": out_grad, "gate_prob": gate_prob, "expert_ids": expert_ids, "w_gate": w_gate, "w_up": w_up, "w_down": w_down}


def rounded(value):
    return lax.optimization_barrier(value.astype(jnp.bfloat16)).astype(jnp.float32)


def expert_rows(tokens_g, grad_g, prob_g, route_g, expert, w_gate_e, w_up_e, w_down_e):
    limit = N_EXPERT * N_SEQ * CAP
    hits = route_g == expert
    picked = jnp.nonzero(hits, size=limit, fill_value=0)[0].astype(jnp.int32)
    live = jnp.arange(limit) < jnp.sum(hits.astype(jnp.int32))
    x_rows = jnp.where(live[:, None], tokens_g[picked], jnp.zeros((), jnp.bfloat16))
    dy_rows = jnp.where(live[:, None], grad_g[picked], jnp.zeros((), jnp.bfloat16))
    p_rows = jnp.where(live, prob_g[picked].astype(jnp.float32), jnp.zeros((), jnp.float32))
    gate_pre = jnp.dot(x_rows, w_gate_e, preferred_element_type=jnp.float32)
    up_pre = jnp.dot(x_rows, w_up_e, preferred_element_type=jnp.float32)
    sigmoid_gate = jax.nn.sigmoid(gate_pre)
    activated = gate_pre * sigmoid_gate
    hidden = activated * up_pre
    hidden_grad = jnp.dot(dy_rows, w_down_e.T, preferred_element_type=jnp.float32)
    scaled_grad = p_rows[:, None] * hidden_grad
    gate_delta = (scaled_grad * up_pre * sigmoid_gate * (1.0 + gate_pre * (1.0 - sigmoid_gate))).astype(jnp.bfloat16)
    up_delta = (scaled_grad * activated).astype(jnp.bfloat16)
    shard_width = H // N_SEQ
    token_part = jnp.zeros((limit, D), jnp.float32)
    gate_part = jnp.zeros((limit,), jnp.float32)
    for block in range(N_SEQ):
        low = block * shard_width
        high = low + shard_width
        partial_value = jnp.dot(gate_delta[:, low:high], w_gate_e[:, low:high].T, preferred_element_type=jnp.float32)
        partial_value = partial_value + jnp.dot(up_delta[:, low:high], w_up_e[:, low:high].T, preferred_element_type=jnp.float32)
        token_part = token_part + rounded(partial_value)
        gate_part = gate_part + rounded(jnp.sum(hidden[:, low:high] * hidden_grad[:, low:high], axis=1))
    hidden_bf = hidden.astype(jnp.bfloat16)
    scaled_dy = (dy_rows.astype(jnp.float32) * p_rows[:, None]).astype(jnp.bfloat16)
    grad_gate = jnp.dot(x_rows.T, gate_delta, preferred_element_type=jnp.float32)
    grad_up = jnp.dot(x_rows.T, up_delta, preferred_element_type=jnp.float32)
    grad_down = jnp.dot(hidden_bf.T, scaled_dy, preferred_element_type=jnp.float32)
    return picked, token_part, gate_part, grad_gate, grad_up, grad_down


def reference(tokens, out_grad, gate_prob, expert_ids, w_gate, w_up, w_down):
    group_rows = TOKENS // N_DP
    token_acc = jnp.zeros((TOKENS, D), jnp.float32)
    router_acc = jnp.zeros((TOKENS,), jnp.float32)
    gate_acc = jnp.zeros((EXPERTS, D, H), jnp.float32)
    up_acc = jnp.zeros((EXPERTS, D, H), jnp.float32)
    down_acc = jnp.zeros((EXPERTS, H, D), jnp.float32)
    for team in range(N_DP):
        low = team * group_rows
        high = low + group_rows
        for expert in range(EXPERTS):
            picked, token_part, gate_part, grad_gate, grad_up, grad_down = expert_rows(
                tokens[low:high], out_grad[low:high], gate_prob[low:high], expert_ids[low:high, 0],
                expert, w_gate[expert], w_up[expert], w_down[expert])
            token_acc = token_acc.at[low + picked].add(token_part)
            router_acc = router_acc.at[low + picked].add(gate_part)
            gate_acc = gate_acc.at[expert].add(rounded(grad_gate))
            up_acc = up_acc.at[expert].add(rounded(grad_up))
            down_acc = down_acc.at[expert].add(rounded(grad_down))
    return (token_acc.astype(jnp.bfloat16), router_acc.astype(jnp.bfloat16), gate_acc.astype(jnp.bfloat16),
            up_acc.astype(jnp.bfloat16), down_acc.astype(jnp.bfloat16))
```

```python
import jax
import jax.numpy as jnp
from jax import lax
from jax.sharding import PartitionSpec as P

TOP = 1
BF = jnp.bfloat16
F32 = jnp.float32
CONTRACT_LAST = (((1,), (1,)), ((), ()))
CONTRACT_FIRST = (((0,), (0,)), ((), ()))


def dot(left, right, dims=(((1,), (0,)), ((), ()))):
    return lax.dot_general(left, right, dims, preferred_element_type=F32)


def send_xor(value, axis, mask):
    size = lax.axis_size(axis)
    return lax.ppermute(value, axis, [(i, i ^ mask) for i in range(size)])


def send_home(value, expert_mask, seq_mask):
    if not expert_mask:
        return send_xor(value, "seq", seq_mask) if seq_mask else value
    if not seq_mask:
        return send_xor(value, "expert", expert_mask)
    seq_count = lax.axis_size("seq")
    total = lax.axis_size("expert") * seq_count
    mask = expert_mask * seq_count + seq_mask
    return lax.ppermute(value, ("expert", "seq"), [(i, i ^ mask) for i in range(total)])


def gather_slots(value):
    count = lax.axis_size("seq")
    if count != 4:
        return [value] + [send_xor(value, "seq", j) for j in range(1, count)]
    place = lax.axis_index("seq")
    inner = (place == 1) | (place == 2)
    middle, outward = [(1, 2), (2, 1)], [(1, 0), (2, 3)]
    first = send_xor(value, "seq", 1)
    across = lax.ppermute(value, "seq", middle)
    relayed = lax.ppermute(first, "seq", middle)
    out_near = lax.ppermute(across, "seq", outward)
    out_far = lax.ppermute(relayed, "seq", outward)
    return [
        value,
        first,
        jnp.where(inner, relayed, out_near),
        jnp.where(inner, across, out_far),
    ]


def sum_over_dp(terms):
    count = lax.axis_size("dp")
    place = lax.axis_index("dp")
    rows = terms.shape[0] // count
    held = terms.reshape((count, rows) + terms.shape[1:])
    mask = 1
    while mask < count:
        split = held.reshape((held.shape[0] // 2, 2) + held.shape[1:])
        bit = (place // mask) % 2
        kept = lax.dynamic_index_in_dim(split, bit, 1, keepdims=False)
        given = lax.dynamic_index_in_dim(split, 1 - bit, 1, keepdims=False)
        taken = send_xor(given, "dp", mask)
        held = (kept.astype(F32) + taken.astype(F32)).astype(BF)
        mask *= 2
    return held[0]


def body(tokens, out_grad, gate_prob, expert_ids, w_gate, w_up, w_down):
    expert_count = lax.axis_size("expert")
    seq_count = lax.axis_size("seq")
    tok_rows, feat_width = tokens.shape
    capacity = tok_rows * TOP * 17 // (16 * expert_count)
    room = -(-capacity // 8) * 8
    my_expert = lax.axis_index("expert")
    route = expert_ids[:, 0]
    onehot = (route[:, None] == jnp.arange(expert_count)[None, :]).astype(F32)
    earlier = (jnp.arange(tok_rows)[:, None] > jnp.arange(tok_rows)[None, :]).astype(F32)
    before = dot(earlier, onehot)
    slot_index = jnp.sum(before * onehot, axis=1).astype(jnp.int32)
    block = jnp.bitwise_xor(route, my_expert)
    target = block * room + slot_index
    prob = gate_prob.astype(F32)

    def placer_of(first, last):
        return (first * room + jnp.arange((last - first) * room))[:, None] == target[None, :]

    def pack(first, last):
        placer = placer_of(first, last)
        scaler = jnp.where(placer, prob[None, :], 0.0).astype(BF)
        return dot(placer.astype(BF), tokens).astype(BF), dot(scaler, out_grad).astype(BF)

    packed = [pack(j, j + 1) for j in range(expert_count)]
    swapped_x = [send_xor(packed[j][0], "expert", j) for j in range(1, expert_count)]
    swapped_dy = [send_xor(packed[j][1], "expert", j) for j in range(1, expert_count)]
    pieces_x = [packed[0][0], jnp.concatenate(swapped_x, axis=0)]
    dy_mine = jnp.concatenate([packed[0][1]] + swapped_dy, axis=0)
    near_x, far_x = [gather_slots(piece) for piece in pieces_x]
    slots_dy = gather_slots(dy_mine)
    slots_x = [jnp.concatenate(pair, axis=0) for pair in zip(near_x, far_x)]

    gate_local, up_local, down_local = w_gate[0], w_up[0], w_down[0]
    home_parts = [[] for _ in range(expert_count)]
    gate_parts, gate_deltas, up_deltas, hiddens = [], [], [], []
    for j in range(seq_count):
        x_rows, dy_rows = slots_x[j], slots_dy[j]
        gate_pre = dot(x_rows, gate_local)
        up_pre = dot(x_rows, up_local)
        sigmoid_gate = jax.nn.sigmoid(gate_pre)
        activated = gate_pre * sigmoid_gate
        hidden = activated * up_pre
        scaled_grad = dot(dy_rows, down_local, CONTRACT_LAST)
        gate_parts.append(jnp.sum(hidden * scaled_grad, axis=1).astype(BF))
        gate_delta = (
            scaled_grad * up_pre * sigmoid_gate * (1.0 + gate_pre * (1.0 - sigmoid_gate))
        ).astype(BF)
        up_delta = (scaled_grad * activated).astype(BF)
        token_part = (
            dot(gate_delta, gate_local, CONTRACT_LAST) + dot(up_delta, up_local, CONTRACT_LAST)
        ).astype(BF)
        for k in range(expert_count):
            part = token_part[k * room : (k + 1) * room]
            home_parts[k].append(send_home(part, k, j))
        gate_deltas.append(gate_delta)
        up_deltas.append(up_delta)
        hiddens.append(hidden.astype(BF))

    all_x = jnp.concatenate(slots_x, axis=0)
    all_dy = jnp.concatenate(slots_dy, axis=0)
    gate_w_grad = sum_over_dp(
        dot(all_x, jnp.concatenate(gate_deltas, axis=0), CONTRACT_FIRST).astype(BF)
    )
    up_w_grad = sum_over_dp(
        dot(all_x, jnp.concatenate(up_deltas, axis=0), CONTRACT_FIRST).astype(BF)
    )
    down_w_grad = sum_over_dp(
        dot(all_dy, jnp.concatenate(hiddens, axis=0), CONTRACT_FIRST).astype(BF)
    )

    my_seq = lax.axis_index("seq")
    parts = jnp.stack(gate_parts).reshape(seq_count, expert_count, room)
    flat = parts.transpose(1, 0, 2).reshape(expert_count * seq_count, room)
    total = expert_count * seq_count
    mine = my_expert * seq_count + my_seq
    order = jnp.bitwise_xor(jnp.arange(total), mine)
    swap = (order[:, None] == jnp.arange(total)[None, :]).astype(BF)
    sent = dot(swap, flat).astype(BF)
    back = lax.all_to_all(sent, ("expert", "seq"), split_axis=0, concat_axis=0, tiled=True)
    back = dot(swap, back).reshape(expert_count, seq_count, room)
    home_g = jnp.sum(back, axis=1).reshape(1, expert_count * room)

    home_x = jnp.concatenate(
        [sum(part.astype(F32) for part in home_parts[k]).astype(BF) for k in range(expert_count)],
        axis=0,
    )
    placer = placer_of(0, expert_count)
    token_grad = dot(placer.astype(BF), home_x, CONTRACT_FIRST).astype(BF)
    gate_grad = (jnp.sum(jnp.where(placer, home_g.T, 0.0), axis=0) / prob).astype(BF)
    return (token_grad, gate_grad, gate_w_grad[None], up_w_grad[None], down_w_grad.T[None])


def solution(mesh):
    placed = (
        P(("dp", "expert", "seq"), None),
        P(("dp", "expert", "seq"), None),
        P(("dp", "expert", "seq")),
        P(("dp", "expert", "seq"), None),
        P("expert", None, "seq"),
        P("expert", None, "seq"),
        P("expert", "seq", None),
    )
    return jax.shard_map(
        body,
        mesh=mesh,
        in_specs=placed,
        out_specs=(
            P(("dp", "expert", "seq"), None),
            P(("dp", "expert", "seq")),
            P("expert", "dp", "seq"),
            P("expert", "dp", "seq"),
            P("expert", "seq", "dp"),
        ),
        check_vma=False,
    )
```

```python
import functools

import jax
import jax.numpy as jnp
from jax import lax
from jax.experimental import pallas as pl
from jax.experimental.pallas import tpu as pltpu
from jax.sharding import PartitionSpec as P

TOP = 1
BF = jnp.bfloat16
F32 = jnp.float32
PLAIN = (((1,), (0,)), ((), ()))
CONTRACT_LAST = (((1,), (1,)), ((), ()))
CONTRACT_FIRST = (((0,), (0,)), ((), ()))
MIDDLE = [(1, 2), (2, 1)]
OUTWARD = [(1, 0), (2, 3)]
INWARD_TWO = [(0, 2), (3, 1)]


def dot(left, right, dims=PLAIN):
    return lax.dot_general(left, right, dims, preferred_element_type=F32)


def after(value, *others):
    return lax.optimization_barrier((value,) + others)[0]


def send_xor(value, axis, mask):
    size = lax.axis_size(axis)
    return lax.ppermute(value, axis, [(i, i ^ mask) for i in range(size)])


def send_home(value, expert_mask, seq_mask):
    if not expert_mask:
        return send_xor(value, "seq", seq_mask) if seq_mask else value
    if not seq_mask:
        return send_xor(value, "expert", expert_mask)
    seq_count = lax.axis_size("seq")
    total = lax.axis_size("expert") * seq_count
    mask = expert_mask * seq_count + seq_mask
    return lax.ppermute(value, ("expert", "seq"), [(i, i ^ mask) for i in range(total)])


def slot_kernel(
    blocks,
    place,
    x,
    dy,
    wg,
    wu,
    wd,
    part,
    far_share,
    near_share,
    own_share,
    kx,
    ky,
    kg,
    ku,
    kd,
    kp,
    kfar,
    knear,
    kown,
    sems,
    out_sems,
):
    feat, width = kg.shape
    rows = kx.shape[0]
    step = feat // blocks
    half, quarter = feat // 2, feat // 4

    def fetch(i):
        cols = pl.ds(i * step, step)
        pairs = [(x, kx, True), (wg, kg, False), (dy, ky, True), (wu, ku, False), (wd, kd, True)]
        return [
            pltpu.make_async_copy(
                source.at[:, cols] if last else source.at[cols],
                target.at[:, cols] if last else target.at[cols],
                sems.at[k, i],
            )
            for k, (source, target, last) in enumerate(pairs)
        ]

    copies = [fetch(i) for i in range(blocks)]
    for group in copies:
        for copy in group:
            copy.start()
    gate_pre = up_pre = scaled_grad = None
    for i in range(blocks):
        for copy in copies[i]:
            copy.wait()
        cols = pl.ds(i * step, step)
        terms = (
            dot(kx[:, cols], kg[cols]),
            dot(kx[:, cols], ku[cols]),
            dot(ky[:, cols], kd[:, cols], CONTRACT_LAST),
        )
        if i == 0:
            gate_pre, up_pre, scaled_grad = terms
        else:
            gate_pre, up_pre, scaled_grad = (
                gate_pre + terms[0],
                up_pre + terms[1],
                scaled_grad + terms[2],
            )
    sigmoid_gate = jax.nn.sigmoid(gate_pre)
    activated = gate_pre * sigmoid_gate
    hidden = activated * up_pre
    gate_part = jnp.sum(hidden * scaled_grad, axis=1, keepdims=True).astype(BF)
    kp[:, feat:] = jnp.broadcast_to(gate_part, (rows, kp.shape[1] - feat))
    gate_delta = (
        scaled_grad * up_pre * sigmoid_gate * (1.0 + gate_pre * (1.0 - sigmoid_gate))
    ).astype(BF)
    up_delta = (scaled_grad * activated).astype(BF)
    hidden = hidden.astype(BF)
    hi, lo = place[0], place[1]
    shares = [
        (kfar, far_share, half, (1 - hi) * half),
        (knear, near_share, quarter, hi * half + (1 - lo) * quarter),
        (kown, own_share, quarter, hi * half + lo * quarter),
    ]
    outs = []
    for keep, share, count, start in shares:
        cols = pl.ds(pl.multiple_of(start, quarter), count)
        keep[:rows, :count] = kx[:, cols]
        keep[:rows, count : 2 * count] = ky[:, cols]
        low = 2 * count
        keep[:rows, low : low + width] = gate_delta
        keep[:rows, low + width : low + 2 * width] = up_delta
        keep[:rows, low + 2 * width : low + 3 * width] = hidden
        if keep.shape[0] > rows:
            keep[rows:] = jnp.zeros((keep.shape[0] - rows, keep.shape[1]), BF)
        copy = pltpu.make_async_copy(keep, share, out_sems.at[len(outs)])
        copy.start()
        outs.append(copy)
    for i in range(blocks):
        cols = pl.ds(i * step, step)
        kp[:, cols] = (
            dot(gate_delta, kg[cols], CONTRACT_LAST) + dot(up_delta, ku[cols], CONTRACT_LAST)
        ).astype(BF)
        if i == blocks - 1:
            cols = pl.ds(i * step, kp.shape[1] - i * step)
        copy = pltpu.make_async_copy(kp.at[:, cols], part.at[:, cols], out_sems.at[len(outs)])
        copy.start()
        outs.append(copy)
    for copy in outs:
        copy.wait()


def slot_work(place, x_rows, dy_rows, gate_local, up_local, down_local):
    rows, feat = x_rows.shape
    width = gate_local.shape[1]
    tall = -(-rows // 16) * 16
    wide = -(-3 * width // 128) * 128
    blocks = 4
    away = pl.BlockSpec(memory_space=pltpu.HBM)
    shares = [(tall, feat + wide), (tall, feat // 2 + wide), (tall, feat // 2 + wide)]
    return pl.pallas_call(
        functools.partial(slot_kernel, blocks),
        out_shape=[jax.ShapeDtypeStruct((rows, feat + 128), BF)]
        + [jax.ShapeDtypeStruct(shape, BF) for shape in shares],
        in_specs=[pl.BlockSpec(memory_space=pltpu.SMEM)] + [away] * 5,
        out_specs=[away] * 4,
        scratch_shapes=[
            pltpu.VMEM((rows, feat), BF),
            pltpu.VMEM((rows, feat), BF),
            pltpu.VMEM((feat, width), BF),
            pltpu.VMEM((feat, width), BF),
            pltpu.VMEM((width, feat), BF),
            pltpu.VMEM((rows, feat + 128), BF),
        ]
        + [pltpu.VMEM(shape, BF) for shape in shares]
        + [
            pltpu.SemaphoreType.DMA((5, blocks)),
            pltpu.SemaphoreType.DMA((3 + blocks,)),
        ],
        compiler_params=pltpu.CompilerParams(vmem_limit_bytes=56 * 1024 * 1024),
        name="slot_work",
    )(place, x_rows, dy_rows, gate_local, up_local, down_local)


def weight_kernel(slots, started, width, *refs):
    place, refs = refs[0], refs[1:]
    sources = [refs[4 * s : 4 * s + 4] for s in range(slots)]
    refs = refs[4 * slots :]
    before, refs = (refs[:3], refs[3:]) if started else (None, refs)
    outs, refs = refs[:3], refs[3:]
    keep_x, keep_dy, keep_d, sums_gu, sums_d, sems = refs
    quarter, wide = keep_x.shape[2], keep_d.shape[2]
    tall = keep_x.shape[1] // 4
    half = 2 * quarter
    low = pl.multiple_of(place[1] * quarter, quarter)
    shifted = pl.multiple_of(half + place[1] * quarter, quarter)
    copies = []
    for s in range(slots):
        own, near, far, cross = sources[s]
        cuts = [
            (own, 0, quarter, half),
            (near, 0, quarter, half),
            (far, low, shifted, 2 * half),
            (cross, low, shifted, 2 * half),
        ]
        for g, (ref, *starts) in enumerate(cuts):
            rows = pl.ds(g * tall, tall)
            for k, (keep, start) in enumerate(zip((keep_x, keep_dy, keep_d), starts)):
                copy = pltpu.make_async_copy(
                    ref.at[:, pl.ds(start, keep.shape[2])],
                    keep.at[s, rows],
                    sems.at[s, 3 * g + k],
                )
                copy.start()
                copies.append((s, copy))
    for s in range(slots):
        for n, copy in copies:
            if n == s:
                copy.wait()
        gate_up = dot(keep_x[s], keep_d[s, :, : 2 * width], CONTRACT_FIRST)
        down = dot(keep_d[s, :, 2 * width : 3 * width], keep_dy[s], CONTRACT_FIRST)
        if s == 0 and started:
            sums_gu[:, :width] = before[0][...] + gate_up[:, :width]
            sums_gu[:, width:] = before[1][...] + gate_up[:, width:]
            sums_d[...] = before[2][...] + down
        elif s == 0:
            sums_gu[...] = gate_up
            sums_d[...] = down
        else:
            sums_gu[...] += gate_up
            sums_d[...] += down
    outs[0][...] = sums_gu[:, :width].astype(outs[0].dtype)
    outs[1][...] = sums_gu[:, width:].astype(outs[1].dtype)
    outs[2][...] = sums_d[...].astype(outs[2].dtype)


def weight_work(place, width, slots, before, dtype):
    tall, both = slots[0][0].shape
    wide = -(-3 * width // 128) * 128
    quarter = (both - wide) // 2
    whole = pl.BlockSpec(memory_space=pltpu.VMEM)
    away = pl.BlockSpec(memory_space=pltpu.HBM)
    shapes = [(quarter, width), (quarter, width), (width, quarter)]
    return pl.pallas_call(
        functools.partial(weight_kernel, len(slots), bool(before), width),
        out_shape=[jax.ShapeDtypeStruct(shape, dtype) for shape in shapes],
        in_specs=[pl.BlockSpec(memory_space=pltpu.SMEM)]
        + [away] * (4 * len(slots))
        + [whole] * len(before),
        out_specs=[whole] * 3,
        scratch_shapes=[
            pltpu.VMEM((len(slots), 4 * tall, quarter), BF),
            pltpu.VMEM((len(slots), 4 * tall, quarter), BF),
            pltpu.VMEM((len(slots), 4 * tall, wide), BF),
            pltpu.VMEM((quarter, 2 * width), F32),
            pltpu.VMEM((width, quarter), F32),
            pltpu.SemaphoreType.DMA((len(slots), 12)),
        ],
        compiler_params=pltpu.CompilerParams(vmem_limit_bytes=56 * 1024 * 1024),
        name="weight_work",
    )(place, *[array for slot in slots for array in slot], *before)


def body(tokens, out_grad, gate_prob, expert_ids, w_gate, w_up, w_down):
    expert_count = lax.axis_size("expert")
    seq_count = lax.axis_size("seq")
    tok_rows, feat_width = tokens.shape
    capacity = tok_rows * TOP * 17 // (16 * expert_count)
    my_expert = lax.axis_index("expert")
    my_seq = lax.axis_index("seq")
    route = expert_ids[:, 0]
    onehot = (route[:, None] == jnp.arange(expert_count)[None, :]).astype(F32)
    earlier = (jnp.arange(tok_rows)[:, None] > jnp.arange(tok_rows)[None, :]).astype(F32)
    before = dot(earlier, onehot)
    slot_index = jnp.sum(before * onehot, axis=1).astype(jnp.int32)
    block = jnp.bitwise_xor(route, my_expert)
    target = block * capacity + slot_index
    prob = gate_prob.astype(F32)

    def placer_of(first, last):
        rows = first * capacity + jnp.arange((last - first) * capacity)
        return rows[:, None] == target[None, :]

    def pack_x(first, last):
        return dot(placer_of(first, last).astype(BF), tokens).astype(BF)

    def pack_dy(first, last):
        scaler = jnp.where(placer_of(first, last), prob[None, :], 0.0).astype(BF)
        return dot(scaler, out_grad).astype(BF)

    def joined(first, rest):
        return jnp.concatenate([first] + list(rest), axis=0)

    gate_local, up_local, down_local = w_gate[0], w_up[0], w_down[0]
    others = range(1, expert_count)
    far_x = [send_xor(pack_x(j, j + 1), "expert", j) for j in others]
    near_x = pack_x(0, 1)
    far_dy = [send_xor(pack_dy(j, j + 1), "expert", j) for j in others]
    near_dy = pack_dy(0, 1)
    far_x = far_x[0] if len(far_x) == 1 else jnp.concatenate(far_x, axis=0)
    slot_x = [joined(near_x, [far_x])]
    slot_dy = [joined(near_dy, far_dy)]

    dp_index = lax.axis_index("dp")
    place = jnp.stack([dp_index // 2, dp_index % 2]).astype(jnp.int32)
    width = gate_local.shape[1]
    token_parts, shares = [], []

    def work(x_rows, dy_rows):
        part, far_share, near_share, own_share = slot_work(
            place, x_rows, dy_rows, gate_local, up_local, down_local
        )
        token_parts.append(part)
        near = send_xor(near_share, "dp", 1)
        far = send_xor(far_share, "dp", 2)
        shares.append([own_share, near, far, send_xor(far, "dp", 1)])
        return part

    if seq_count == 4:
        inner = (my_seq == 1) | (my_seq == 2)
        first_near = send_xor(near_x, "seq", 1)
        across_near = lax.ppermute(near_x, "seq", MIDDLE)
        first_far = send_xor(far_x, "seq", 1)
        across_far = lax.ppermute(far_x, "seq", MIDDLE)
        dy_first = send_xor(slot_dy[0], "seq", 1)
        dy_across = lax.ppermute(slot_dy[0], "seq", MIDDLE)
        x_first = joined(first_near, [first_far])
        x_across = joined(across_near, [across_far])
        done = work(after(slot_x[0], x_first), slot_dy[0])
        x_relayed = lax.ppermute(after(x_first, x_across), "seq", MIDDLE)
        x_near = lax.ppermute(after(x_across, x_first), "seq", OUTWARD)
        dy_relayed = lax.ppermute(after(dy_first, dy_across, done), "seq", MIDDLE)
        dy_near = lax.ppermute(after(dy_across, dy_first, done), "seq", OUTWARD)
        done = work(after(x_first, x_relayed, shares[0][2]), dy_first)
        x_far = lax.ppermute(after(x_relayed, x_near), "seq", OUTWARD)
        work(
            jnp.where(inner, x_relayed, x_near),
            jnp.where(inner, dy_relayed, dy_near),
        )
        dy_far = lax.ppermute(after(dy_relayed, dy_near, done), "seq", OUTWARD)
        over = lax.ppermute(token_parts[2], "seq", MIDDLE)
        two_away = lax.ppermute(token_parts[2], "seq", INWARD_TWO)
        onward = (token_parts[1].astype(F32) + over.astype(F32)).astype(BF)
        one_away = send_xor(onward, "seq", 1)
        work(
            jnp.where(inner, x_across, after(x_far, onward, shares[1][2])),
            jnp.where(inner, dy_across, dy_far),
        )
        so_far = weight_work(place, width, shares[:2], [], F32)
        early = [token_parts[0], two_away, after(one_away, so_far[0])]
    else:
        work(slot_x[0], slot_dy[0])
        for j in range(1, seq_count):
            work(send_xor(slot_x[0], "seq", j), send_xor(slot_dy[0], "seq", j))
        so_far = weight_work(place, width, shares[:2], [], F32)
        early = [token_parts[0]]
        early += [send_xor(token_parts[j], "seq", j) for j in range(1, seq_count - 1)]
    for j in range(2, seq_count - 2, 2):
        so_far = weight_work(place, width, shares[j : j + 2], so_far, F32)
    gate_w_grad, up_w_grad, down_w_grad = weight_work(place, width, shares[-2:], so_far, BF)
    last = seq_count - 1
    early = sum(part.astype(F32) for part in early)

    def rows_of(array, k):
        return array[k * capacity : (k + 1) * capacity]

    homes = []
    for k in range(expert_count):
        direct = send_home(rows_of(token_parts[last], k), k, last)
        first = rows_of(early, k)
        if k:
            first = send_xor(first.astype(BF), "expert", k).astype(F32)
        homes.append((first + direct.astype(F32)).astype(BF))
    home_x = jnp.concatenate(homes, axis=0)

    placer = placer_of(0, expert_count)
    placer = placer.astype(BF)
    token_grad = dot(placer, home_x[:, :feat_width], CONTRACT_FIRST).astype(BF)
    home_g = dot(placer, home_x[:, feat_width:], CONTRACT_FIRST)[:, 0]
    gate_grad = (home_g / prob).astype(BF)
    return (token_grad, gate_grad, gate_w_grad[None], up_w_grad[None], down_w_grad[None])


def solution(mesh):
    placed = (
        P(("dp", "expert", "seq"), None),
        P(("dp", "expert", "seq"), None),
        P(("dp", "expert", "seq")),
        P(("dp", "expert", "seq"), None),
        P("expert", None, "seq"),
        P("expert", None, "seq"),
        P("expert", "seq", None),
    )
    return jax.shard_map(
        body,
        mesh=mesh,
        in_specs=placed,
        out_specs=(
            P(("dp", "expert", "seq"), None),
            P(("dp", "expert", "seq")),
            P("expert", "dp", "seq"),
            P("expert", "dp", "seq"),
            P("expert", "seq", "dp"),
        ),
        check_vma=False,
    )
```

```python
import functools

import jax
import jax.numpy as jnp
from jax import lax
from jax.experimental import pallas as pl
from jax.experimental.pallas import tpu as pltpu
from jax.sharding import PartitionSpec as P

TOP = 1
BF = jnp.bfloat16
F32 = jnp.float32
PLAIN = (((1,), (0,)), ((), ()))
CONTRACT_LAST = (((1,), (1,)), ((), ()))
CONTRACT_FIRST = (((0,), (0,)), ((), ()))
MIDDLE = [(1, 2), (2, 1)]
OUTWARD = [(1, 0), (2, 3)]
INWARD = [(0, 1), (3, 2)]


def dot(left, right, dims=PLAIN):
    return lax.dot_general(left, right, dims, preferred_element_type=F32)


def after(value, *others):
    return lax.optimization_barrier((value,) + others)[0]


def send_xor(value, axis, mask):
    size = lax.axis_size(axis)
    return lax.ppermute(value, axis, [(i, i ^ mask) for i in range(size)])


def send_home(value, expert_mask, seq_mask):
    if not expert_mask:
        return send_xor(value, "seq", seq_mask) if seq_mask else value
    if not seq_mask:
        return send_xor(value, "expert", expert_mask)
    seq_count = lax.axis_size("seq")
    total = lax.axis_size("expert") * seq_count
    mask = expert_mask * seq_count + seq_mask
    return lax.ppermute(value, ("expert", "seq"), [(i, i ^ mask) for i in range(total)])


def slot_kernel(
    blocks,
    place,
    x,
    dy,
    wg,
    wu,
    wd,
    part,
    far_share,
    own_share,
    kx,
    ky,
    kg,
    ku,
    kd,
    kp,
    kfar,
    kown,
    sems,
    out_sems,
):
    feat, width = kg.shape
    rows = kx.shape[0]
    step = feat // blocks
    half = feat // 2

    def fetch(i):
        cols = pl.ds(i * step, step)
        pairs = [(x, kx, True), (wg, kg, False), (dy, ky, True), (wu, ku, False), (wd, kd, True)]
        return [
            pltpu.make_async_copy(
                source.at[:, cols] if last else source.at[cols],
                target.at[:, cols] if last else target.at[cols],
                sems.at[k, i],
            )
            for k, (source, target, last) in enumerate(pairs)
        ]

    copies = [fetch(i) for i in range(blocks)]
    for group in copies:
        for copy in group:
            copy.start()
    gate_pre = up_pre = scaled_grad = None
    for i in range(blocks):
        for copy in copies[i]:
            copy.wait()
        cols = pl.ds(i * step, step)
        terms = (
            dot(kx[:, cols], kg[cols]),
            dot(kx[:, cols], ku[cols]),
            dot(ky[:, cols], kd[:, cols], CONTRACT_LAST),
        )
        if i == 0:
            gate_pre, up_pre, scaled_grad = terms
        else:
            gate_pre, up_pre, scaled_grad = (
                gate_pre + terms[0],
                up_pre + terms[1],
                scaled_grad + terms[2],
            )
    sigmoid_gate = jax.nn.sigmoid(gate_pre)
    activated = gate_pre * sigmoid_gate
    hidden = activated * up_pre
    gate_part = jnp.sum(hidden * scaled_grad, axis=1, keepdims=True).astype(BF)
    kp[:, feat:] = jnp.broadcast_to(gate_part, (rows, kp.shape[1] - feat))
    gate_delta = (
        scaled_grad * up_pre * sigmoid_gate * (1.0 + gate_pre * (1.0 - sigmoid_gate))
    ).astype(BF)
    up_delta = (scaled_grad * activated).astype(BF)
    hidden = hidden.astype(BF)
    outs = []
    for keep, share, side in [(kfar, far_share, 1 - place[0]), (kown, own_share, place[0])]:
        count = half
        cols = pl.ds(pl.multiple_of(side * half, half), half)
        keep[:rows, :count] = kx[:, cols]
        keep[:rows, count : 2 * count] = ky[:, cols]
        low = 2 * count
        keep[:rows, low : low + width] = gate_delta
        keep[:rows, low + width : low + 2 * width] = up_delta
        keep[:rows, low + 2 * width : low + 3 * width] = hidden
        if keep.shape[0] > rows:
            keep[rows:] = jnp.zeros((keep.shape[0] - rows, keep.shape[1]), BF)
        copy = pltpu.make_async_copy(keep, share, out_sems.at[len(outs)])
        copy.start()
        outs.append(copy)
    for i in range(blocks):
        cols = pl.ds(i * step, step)
        kp[:, cols] = (
            dot(gate_delta, kg[cols], CONTRACT_LAST) + dot(up_delta, ku[cols], CONTRACT_LAST)
        ).astype(BF)
        if i == blocks - 1:
            cols = pl.ds(i * step, kp.shape[1] - i * step)
        copy = pltpu.make_async_copy(kp.at[:, cols], part.at[:, cols], out_sems.at[len(outs)])
        copy.start()
        outs.append(copy)
    for copy in outs:
        copy.wait()


def slot_work(place, x_rows, dy_rows, gate_local, up_local, down_local):
    rows, feat = x_rows.shape
    width = gate_local.shape[1]
    tall = -(-rows // 16) * 16
    wide = -(-3 * width // 128) * 128
    blocks = 4
    away = pl.BlockSpec(memory_space=pltpu.HBM)
    shares = [(tall, feat + wide), (tall, feat + wide)]
    return pl.pallas_call(
        functools.partial(slot_kernel, blocks),
        out_shape=[jax.ShapeDtypeStruct((rows, feat + 128), BF)]
        + [jax.ShapeDtypeStruct(shape, BF) for shape in shares],
        in_specs=[pl.BlockSpec(memory_space=pltpu.SMEM)] + [away] * 5,
        out_specs=[away] * 3,
        scratch_shapes=[
            pltpu.VMEM((rows, feat), BF),
            pltpu.VMEM((rows, feat), BF),
            pltpu.VMEM((feat, width), BF),
            pltpu.VMEM((feat, width), BF),
            pltpu.VMEM((width, feat), BF),
            pltpu.VMEM((rows, feat + 128), BF),
        ]
        + [pltpu.VMEM(shape, BF) for shape in shares]
        + [
            pltpu.SemaphoreType.DMA((5, blocks)),
            pltpu.SemaphoreType.DMA((2 + blocks,)),
        ],
        compiler_params=pltpu.CompilerParams(vmem_limit_bytes=56 * 1024 * 1024),
        name="slot_work",
    )(place, x_rows, dy_rows, gate_local, up_local, down_local)


def weight_kernel(count, width, *refs):
    place, shares, refs = refs[0], refs[1 : 1 + count], refs[1 + count :]
    keep_gu, give_gu, keep_d, give_d, rows, sums_gu, sums_d, sems = refs
    quarter = sums_gu.shape[1]
    half = 2 * quarter
    tall = rows.shape[0] // count
    copies = [
        pltpu.make_async_copy(share, rows.at[pl.ds(n * tall, tall)], sems.at[n])
        for n, share in enumerate(shares)
    ]
    for copy in copies:
        copy.start()
    for copy in copies:
        copy.wait()
    low = 2 * half
    cut = quarter // 2
    for q in range(2):
        for c in range(2):
            x_cols = pl.ds(q * quarter + c * cut, cut)
            dy_cols = pl.ds(half + q * quarter + c * cut, cut)
            cols = pl.ds(c * cut, cut)
            sums_gu[q, cols] = dot(
                rows[:, x_cols], rows[:, low : low + 2 * width], CONTRACT_FIRST
            ).astype(BF)
            sums_d[q, :, cols] = dot(
                rows[:, low + 2 * width : low + 3 * width], rows[:, dy_cols], CONTRACT_FIRST
            ).astype(BF)
    mine = place[1]
    copies = [
        pltpu.make_async_copy(sums_gu.at[1 - mine], give_gu, sems.at[0]),
        pltpu.make_async_copy(sums_d.at[1 - mine], give_d, sems.at[1]),
        pltpu.make_async_copy(sums_gu.at[mine], keep_gu, sems.at[2]),
        pltpu.make_async_copy(sums_d.at[mine], keep_d, sems.at[3]),
    ]
    for copy in copies:
        copy.start()
    for copy in copies:
        copy.wait()


def weight_work(place, width, shares):
    tall, both = shares[0].shape
    wide = -(-3 * width // 128) * 128
    quarter = (both - wide) // 4
    count = len(shares)
    away = pl.BlockSpec(memory_space=pltpu.HBM)
    shapes = [(quarter, 2 * width), (quarter, 2 * width), (width, quarter), (width, quarter)]
    keep_gu, give_gu, keep_d, give_d = pl.pallas_call(
        functools.partial(weight_kernel, count, width),
        out_shape=[jax.ShapeDtypeStruct(shape, BF) for shape in shapes],
        in_specs=[pl.BlockSpec(memory_space=pltpu.SMEM)] + [away] * count,
        out_specs=[away] * 4,
        scratch_shapes=[
            pltpu.VMEM((count * tall, both), BF),
            pltpu.VMEM((2, quarter, 2 * width), BF),
            pltpu.VMEM((2, width, quarter), BF),
            pltpu.SemaphoreType.DMA((max(count, 4),)),
        ],
        compiler_params=pltpu.CompilerParams(vmem_limit_bytes=56 * 1024 * 1024),
        name="weight_work",
    )(place, *shares)
    return (keep_gu, keep_d), (give_gu, give_d)


def body(tokens, out_grad, gate_prob, expert_ids, w_gate, w_up, w_down):
    expert_count = lax.axis_size("expert")
    seq_count = lax.axis_size("seq")
    tok_rows, feat_width = tokens.shape
    capacity = tok_rows * TOP * 17 // (16 * expert_count)
    my_expert = lax.axis_index("expert")
    my_seq = lax.axis_index("seq")
    route = expert_ids[:, 0]
    onehot = (route[:, None] == jnp.arange(expert_count)[None, :]).astype(F32)
    earlier = (jnp.arange(tok_rows)[:, None] > jnp.arange(tok_rows)[None, :]).astype(F32)
    before = dot(earlier, onehot)
    slot_index = jnp.sum(before * onehot, axis=1).astype(jnp.int32)
    block = jnp.bitwise_xor(route, my_expert)
    target = block * capacity + slot_index
    prob = gate_prob.astype(F32)

    def placer_of(first, last):
        rows = first * capacity + jnp.arange((last - first) * capacity)
        return rows[:, None] == target[None, :]

    def pack_x(first, last):
        return dot(placer_of(first, last).astype(BF), tokens).astype(BF)

    def pack_dy(first, last):
        scaler = jnp.where(placer_of(first, last), prob[None, :], 0.0).astype(BF)
        return dot(scaler, out_grad).astype(BF)

    def joined(first, rest):
        return jnp.concatenate([first] + list(rest), axis=0)

    gate_local, up_local, down_local = w_gate[0], w_up[0], w_down[0]
    others = range(1, expert_count)
    far_x = [pack_x(j, j + 1) for j in others]
    near_x = after(pack_x(0, 1), *far_x)
    out_grad = after(out_grad, near_x)
    far_x = [send_xor(far_x[j - 1], "expert", j) for j in others]
    far_dy = [send_xor(pack_dy(j, j + 1), "expert", j) for j in others]
    near_dy = pack_dy(0, 1)
    far_x = far_x[0] if len(far_x) == 1 else jnp.concatenate(far_x, axis=0)
    slot_x = [joined(near_x, [far_x])]
    slot_dy = [joined(near_dy, far_dy)]

    dp_index = lax.axis_index("dp")
    place = jnp.stack([dp_index // 2, dp_index % 2]).astype(jnp.int32)
    width = gate_local.shape[1]
    token_parts, shares, sums = [], [], []

    def work(x_rows, dy_rows):
        part, far_share, own_share = slot_work(
            place, x_rows, dy_rows, gate_local, up_local, down_local
        )
        token_parts.append(part)
        far = send_xor(after(far_share, shares[-1][1]) if shares else far_share, "dp", 2)
        shares.append([own_share, far])
        return part

    if seq_count == 4:
        inner = (my_seq == 1) | (my_seq == 2)
        first_near = send_xor(near_x, "seq", 1)
        across_near = lax.ppermute(near_x, "seq", MIDDLE)
        first_far = send_xor(far_x, "seq", 1)
        across_far = lax.ppermute(far_x, "seq", MIDDLE)
        dy_first = send_xor(slot_dy[0], "seq", 1)
        dy_across = lax.ppermute(after(slot_dy[0], across_far), "seq", MIDDLE)
        x_first = joined(first_near, [first_far])
        x_across = joined(across_near, [across_far])
        done = work(after(slot_x[0], x_first, x_across), slot_dy[0])
        x_relayed = lax.ppermute(after(x_first, x_across), "seq", MIDDLE)
        x_near = lax.ppermute(after(x_across, x_first), "seq", OUTWARD)
        dy_relayed = lax.ppermute(after(dy_first, dy_across, done), "seq", MIDDLE)
        dy_near = lax.ppermute(after(dy_across, dy_first, done), "seq", OUTWARD)
        done = work(x_first, dy_first)
        x_far = lax.ppermute(after(x_relayed, x_near, done), "seq", OUTWARD)
        dy_far = lax.ppermute(after(dy_relayed, dy_near), "seq", OUTWARD)
        work(
            jnp.where(inner, x_relayed, x_near),
            jnp.where(inner, dy_relayed, dy_near),
        )
        sent = after(token_parts[2], shares[1][1], x_far)
        over = lax.ppermute(sent, "seq", MIDDLE)
        into = lax.ppermute(sent, "seq", INWARD)
        work(
            jnp.where(inner, x_across, after(x_far, shares[2][1])),
            jnp.where(inner, dy_across, dy_far),
        )
        onward = after(token_parts[1], token_parts[3]).astype(F32) + over.astype(F32)
        token_parts[3] = (token_parts[3].astype(F32) + into.astype(F32)).astype(BF)
        returned = [(token_parts[0], 0), (onward.astype(BF), 1), (token_parts[3], 3)]
    else:
        work(slot_x[0], slot_dy[0])
        for j in range(1, seq_count):
            work(send_xor(slot_x[0], "seq", j), send_xor(slot_dy[0], "seq", j))
        returned = [(token_parts[j], j) for j in range(seq_count)]
    kept, given = weight_work(place, width, shares[0] + shares[1])
    sums += [kept, [send_xor(part, "dp", 1) for part in given]]
    homes = []
    for k in range(expert_count):
        rows = slice(k * capacity, (k + 1) * capacity)
        parts = [send_home(part[rows], k, j) for part, j in returned]
        homes.append(sum(part.astype(F32) for part in parts).astype(BF))
    home_x = jnp.concatenate(homes, axis=0)

    for j in range(2, seq_count, 2):
        kept, given = weight_work(place, width, shares[j] + shares[j + 1])
        sums += [kept, [send_xor(part, "dp", 1) for part in given]]
    gate_up = sum(pair[0].astype(F32) for pair in sums).astype(BF)
    down_w_grad = sum(pair[1].astype(F32) for pair in sums).astype(BF)
    gate_w_grad, up_w_grad = gate_up[:, :width], gate_up[:, width:]

    placer = placer_of(0, expert_count)
    placer = placer.astype(BF)
    token_grad = dot(placer, home_x[:, :feat_width], CONTRACT_FIRST).astype(BF)
    home_g = dot(placer, home_x[:, feat_width:], CONTRACT_FIRST)[:, 0]
    gate_grad = (home_g / prob).astype(BF)
    return (token_grad, gate_grad, gate_w_grad[None], up_w_grad[None], down_w_grad[None])


def solution(mesh):
    placed = (
        P(("dp", "expert", "seq"), None),
        P(("dp", "expert", "seq"), None),
        P(("dp", "expert", "seq")),
        P(("dp", "expert", "seq"), None),
        P("expert", None, "seq"),
        P("expert", None, "seq"),
        P("expert", "seq", None),
    )
    return jax.shard_map(
        body,
        mesh=mesh,
        in_specs=placed,
        out_specs=(
            P(("dp", "expert", "seq"), None),
            P(("dp", "expert", "seq")),
            P("expert", "dp", "seq"),
            P("expert", "dp", "seq"),
            P("expert", "seq", "dp"),
        ),
        check_vma=False,
    )
```

```python
import functools

import jax
import jax.numpy as jnp
from jax import lax
from jax.experimental import pallas as pl
from jax.experimental.pallas import tpu as pltpu
from jax.sharding import PartitionSpec as P

TOP = 1
BF = jnp.bfloat16
F32 = jnp.float32
PLAIN = (((1,), (0,)), ((), ()))
CONTRACT_LAST = (((1,), (1,)), ((), ()))
CONTRACT_FIRST = (((0,), (0,)), ((), ()))
MIDDLE = [(1, 2), (2, 1)]
OUTWARD = [(1, 0), (2, 3)]
INWARD = [(0, 1), (3, 2)]


def dot(left, right, dims=PLAIN):
    return lax.dot_general(left, right, dims, preferred_element_type=F32)


def after(value, *others):
    return lax.optimization_barrier((value,) + others)[0]


def send_xor(value, axis, mask):
    size = lax.axis_size(axis)
    return lax.ppermute(value, axis, [(i, i ^ mask) for i in range(size)])


def send_home(value, expert_mask, seq_mask):
    if not expert_mask:
        return send_xor(value, "seq", seq_mask) if seq_mask else value
    if not seq_mask:
        return send_xor(value, "expert", expert_mask)
    seq_count = lax.axis_size("seq")
    total = lax.axis_size("expert") * seq_count
    mask = expert_mask * seq_count + seq_mask
    return lax.ppermute(value, ("expert", "seq"), [(i, i ^ mask) for i in range(total)])


def slot_kernel(blocks, count, choices, place, *refs):
    xs, refs = refs[: count * choices], refs[count * choices :]
    dys, refs = refs[: count * choices], refs[count * choices :]
    wg, wu, wd, refs = refs[0], refs[1], refs[2], refs[3:]
    parts, refs = refs[:count], refs[count:]
    far_share, refs = refs[0], refs[1:]
    own_shares, refs = refs[:count], refs[count:]
    kx, ky, kg, ku, kd, kp, kfar, kown, sems, out_sems = refs
    feat, width = kg.shape
    rows = kx.shape[1]
    step = feat // blocks
    half = feat // 2
    low = 2 * half
    wide = kown.shape[2] - low

    def weights(i):
        cols = pl.ds(i * step, step)
        pairs = [(wg.at[cols], kg.at[cols]), (wu.at[cols], ku.at[cols])]
        return pairs + [(wd.at[:, cols], kd.at[:, cols])]

    def tokens(i, choice):
        cols = pl.ds(i * step, step)
        pairs = []
        for n in range(count):
            pairs += [(xs[n * choices + choice].at[:, cols], kx.at[n, :, cols])]
            pairs += [(dys[n * choices + choice].at[:, cols], ky.at[n, :, cols])]
        return pairs

    def copies_of(i, pairs, first):
        return [
            pltpu.make_async_copy(source, target, sems.at[first + k, i])
            for k, (source, target) in enumerate(pairs)
        ]

    def start_tokens(choice):
        for i in range(blocks):
            for copy in copies_of(i, tokens(i, choice), 3):
                copy.start()

    for i in range(blocks):
        for copy in copies_of(i, weights(i), 0):
            copy.start()
        if i == 0:
            if choices == 1:
                start_tokens(0)
            else:
                for choice in range(choices):
                    pl.when(place[2] == choice)(functools.partial(start_tokens, choice))
    copies = [copies_of(i, weights(i), 0) + copies_of(i, tokens(i, 0), 3) for i in range(blocks)]
    sums = [None] * count
    for i in range(blocks):
        for copy in copies[i]:
            copy.wait()
        cols = pl.ds(i * step, step)
        for n in range(count):
            terms = (
                dot(kx[n, :, cols], kg[cols]),
                dot(kx[n, :, cols], ku[cols]),
                dot(ky[n, :, cols], kd[:, cols], CONTRACT_LAST),
            )
            sums[n] = [s + t for s, t in zip(sums[n], terms)] if i else terms
    outs = []
    backward = []
    side = place[0]
    mine = pl.ds(pl.multiple_of(side * half, half), half)
    other = pl.ds(pl.multiple_of((1 - side) * half, half), half)
    if kfar.shape[0] > rows:
        kfar[rows:] = jnp.zeros((kfar.shape[0] - rows, kfar.shape[1]), BF)
    for n in range(count):
        gate_pre, up_pre, scaled_grad = sums[n]
        sigmoid_gate = jax.nn.sigmoid(gate_pre)
        activated = gate_pre * sigmoid_gate
        hidden = activated * up_pre
        gate_part = jnp.sum(hidden * scaled_grad, axis=1, keepdims=True).astype(BF)
        kp[n, :, feat:] = jnp.broadcast_to(gate_part, (rows, kp.shape[2] - feat))
        gate_delta = (
            scaled_grad * up_pre * sigmoid_gate * (1.0 + gate_pre * (1.0 - sigmoid_gate))
        ).astype(BF)
        up_delta = (scaled_grad * activated).astype(BF)
        backward.append((gate_delta, up_delta))
        kown[n, :rows, :half] = kx[n, :, mine]
        kown[n, :rows, half:low] = ky[n, :, mine]
        last = n == count - 1
        if last:
            kfar[:rows, :half] = kx[n, :, other]
            kfar[:rows, half:low] = ky[n, :, other]
        start = low if last else low + (n + 1) * wide
        for k, delta in enumerate((gate_delta, up_delta, hidden.astype(BF))):
            kown[n, :rows, low + k * width : low + (k + 1) * width] = delta
            kfar[:rows, start + k * width : start + (k + 1) * width] = delta
        if kown.shape[1] > rows:
            kown[n, rows:] = jnp.zeros((kown.shape[1] - rows, kown.shape[2]), BF)
        outs.append(pltpu.make_async_copy(kown.at[n], own_shares[n], out_sems.at[len(outs)]))
        outs[-1].start()
    outs.append(pltpu.make_async_copy(kfar, far_share, out_sems.at[len(outs)]))
    outs[-1].start()
    for i in range(blocks):
        cols = pl.ds(i * step, step)
        taken = pl.ds(i * step, kp.shape[2] - i * step) if i == blocks - 1 else cols
        for n, (gate_delta, up_delta) in enumerate(backward):
            kp[n, :, cols] = (
                dot(gate_delta, kg[cols], CONTRACT_LAST) + dot(up_delta, ku[cols], CONTRACT_LAST)
            ).astype(BF)
            outs.append(
                pltpu.make_async_copy(
                    kp.at[n, :, taken], parts[n].at[:, taken], out_sems.at[len(outs)]
                )
            )
            outs[-1].start()
    for copy in outs:
        copy.wait()


def slot_work(place, xs, dys, gate_local, up_local, down_local):
    rows, feat = xs[0][0].shape
    count, choices = len(xs), len(xs[0])
    width = gate_local.shape[1]
    tall = -(-rows // 16) * 16
    wide = -(-3 * width // 128) * 128
    blocks = 4
    away = pl.BlockSpec(memory_space=pltpu.HBM)
    far_shape, own_shape = (tall, feat + count * wide), (tall, feat + wide)
    outs = pl.pallas_call(
        functools.partial(slot_kernel, blocks, count, choices),
        out_shape=[jax.ShapeDtypeStruct((rows, feat + 128), BF)] * count
        + [jax.ShapeDtypeStruct(far_shape, BF)]
        + [jax.ShapeDtypeStruct(own_shape, BF)] * count,
        in_specs=[pl.BlockSpec(memory_space=pltpu.SMEM)] + [away] * (2 * count * choices + 3),
        out_specs=[away] * (2 * count + 1),
        scratch_shapes=[
            pltpu.VMEM((count, rows, feat), BF),
            pltpu.VMEM((count, rows, feat), BF),
            pltpu.VMEM((feat, width), BF),
            pltpu.VMEM((feat, width), BF),
            pltpu.VMEM((width, feat), BF),
            pltpu.VMEM((count, rows, feat + 128), BF),
            pltpu.VMEM(far_shape, BF),
            pltpu.VMEM((count,) + own_shape, BF),
            pltpu.SemaphoreType.DMA((3 + 2 * count, blocks)),
            pltpu.SemaphoreType.DMA((1 + count + count * blocks,)),
        ],
        compiler_params=pltpu.CompilerParams(vmem_limit_bytes=56 * 1024 * 1024),
        name="slot_work",
    )(place, *sum(xs, []), *sum(dys, []), gate_local, up_local, down_local)
    return outs[:count], outs[count], outs[count + 1 :]


def weight_kernel(cuts, started, width, place, *refs):
    arrays, refs = refs[: len(cuts)], refs[len(cuts) :]
    before, refs = (refs[:4], refs[4:]) if started else ([], refs)
    outs, refs = refs[:4], refs[4:]
    rows, sums_gu, sums_d, old_gu, old_d, sems, old_sems = refs
    quarter = sums_gu.shape[1]
    half = 2 * quarter
    low = 2 * half
    mine = place[1]
    tall = arrays[0].shape[0]
    copies = []
    for array, pieces in zip(arrays, cuts):
        for block, start, target, size in pieces:
            copies.append(
                pltpu.make_async_copy(
                    array.at[:, pl.ds(start, size)],
                    rows.at[pl.ds(block * tall, tall), pl.ds(target, size)],
                    sems.at[len(copies)],
                )
            )
    places = [(mine, 0), (mine, 1), (1 - mine, 0), (1 - mine, 1)]
    for k, ref in enumerate(before):
        side, kind = places[k]
        copies.append(
            pltpu.make_async_copy(ref, (old_gu, old_d)[kind].at[side], old_sems.at[k])
        )
    for copy in copies:
        copy.start()
    for copy in copies:
        copy.wait()
    cut = quarter // 2
    for q in range(2):
        for c in range(2):
            x_cols = pl.ds(q * quarter + c * cut, cut)
            dy_cols = pl.ds(half + q * quarter + c * cut, cut)
            cols = pl.ds(c * cut, cut)
            gate_up = dot(rows[:, x_cols], rows[:, low : low + 2 * width], CONTRACT_FIRST)
            hidden = rows[:, low + 2 * width : low + 3 * width]
            down = dot(hidden, rows[:, dy_cols], CONTRACT_FIRST)
            if started:
                gate_up += old_gu[q, cols].astype(F32)
                down += old_d[q, :, cols].astype(F32)
            sums_gu[q, cols] = gate_up.astype(BF)
            sums_d[q, :, cols] = down.astype(BF)
    copies = [
        pltpu.make_async_copy((sums_gu, sums_d)[kind].at[side], outs[k], old_sems.at[k])
        for k, (side, kind) in enumerate(places)
    ]
    for copy in copies:
        copy.start()
    for copy in copies:
        copy.wait()


def weight_work(place, width, feat, sources, before):
    tall = sources[0][0].shape[0]
    wide = -(-3 * width // 128) * 128
    quarter = feat // 4
    arrays = [array for array, _ in sources]
    cuts = [pieces for _, pieces in sources]
    count = 1 + max(piece[0] for pieces in cuts for piece in pieces)
    away = pl.BlockSpec(memory_space=pltpu.HBM)
    shapes = [(quarter, 2 * width), (width, quarter)] * 2
    kept = [(2,) + shape for shape in shapes[:2]]
    return pl.pallas_call(
        functools.partial(weight_kernel, cuts, bool(before), width),
        out_shape=[jax.ShapeDtypeStruct(shape, BF) for shape in shapes],
        in_specs=[pl.BlockSpec(memory_space=pltpu.SMEM)]
        + [away] * (len(arrays) + len(before)),
        out_specs=[away] * 4,
        scratch_shapes=[pltpu.VMEM((count * tall, feat + wide), BF)]
        + [pltpu.VMEM(shape, BF) for shape in kept * 2]
        + [
            pltpu.SemaphoreType.DMA((sum(len(pieces) for pieces in cuts),)),
            pltpu.SemaphoreType.DMA((4,)),
        ],
        compiler_params=pltpu.CompilerParams(vmem_limit_bytes=56 * 1024 * 1024),
        name="weight_work",
    )(place, *arrays, *before)


def body(tokens, out_grad, gate_prob, expert_ids, w_gate, w_up, w_down):
    expert_count = lax.axis_size("expert")
    seq_count = lax.axis_size("seq")
    tok_rows, feat_width = tokens.shape
    capacity = tok_rows * TOP * 17 // (16 * expert_count)
    my_expert = lax.axis_index("expert")
    my_seq = lax.axis_index("seq")
    route = expert_ids[:, 0]
    onehot = (route[:, None] == jnp.arange(expert_count)[None, :]).astype(F32)
    earlier = (jnp.arange(tok_rows)[:, None] > jnp.arange(tok_rows)[None, :]).astype(F32)
    before = dot(earlier, onehot)
    slot_index = jnp.sum(before * onehot, axis=1).astype(jnp.int32)
    block = jnp.bitwise_xor(route, my_expert)
    target = block * capacity + slot_index
    prob = gate_prob.astype(F32)

    def placer_of(first, last):
        rows = first * capacity + jnp.arange((last - first) * capacity)
        return rows[:, None] == target[None, :]

    def pack_x(first, last):
        return dot(placer_of(first, last).astype(BF), tokens).astype(BF)

    def pack_dy(first, last):
        scaler = jnp.where(placer_of(first, last), prob[None, :], 0.0).astype(BF)
        return dot(scaler, out_grad).astype(BF)

    def joined(first, rest):
        return jnp.concatenate([first] + list(rest), axis=0)

    gate_local, up_local, down_local = w_gate[0], w_up[0], w_down[0]
    others = range(1, expert_count)
    far_x = [pack_x(j, j + 1) for j in others]
    near_x = after(pack_x(0, 1), *far_x)
    out_grad = after(out_grad, near_x)
    far_x = [send_xor(far_x[j - 1], "expert", j) for j in others]
    far_dy = [send_xor(after(pack_dy(j, j + 1), *far_x), "expert", j) for j in others]
    near_dy = pack_dy(0, 1)
    far_x = far_x[0] if len(far_x) == 1 else jnp.concatenate(far_x, axis=0)
    slot_x = [joined(near_x, [far_x])]
    slot_dy = [joined(near_dy, far_dy)]

    dp_index = lax.axis_index("dp")
    is_inner = (my_seq > 0) & (my_seq < seq_count - 1)
    place = jnp.stack([dp_index // 2, dp_index % 2, is_inner]).astype(jnp.int32)
    width = gate_local.shape[1]
    wide = -(-3 * width // 128) * 128
    both = feat_width + wide
    half = feat_width // 2
    tall = -(-expert_count * capacity // 16) * 16

    def work(xs, dys, *others):
        parts, far_share, own_shares = slot_work(
            place, xs, dys, gate_local, up_local, down_local
        )
        far = send_xor(after(far_share, *others), "dp", 2)
        return parts, far, own_shares

    def whole(block):
        return (block, 0, 0, both)

    def rows_of(array, k):
        return array[k * capacity : (k + 1) * capacity]

    if seq_count == 4:
        first_near = send_xor(near_x, "seq", 1)
        across_near = lax.ppermute(near_x, "seq", MIDDLE)
        first_far = send_xor(far_x, "seq", 1)
        across_far = lax.ppermute(far_x, "seq", MIDDLE)
        dy_first = send_xor(slot_dy[0], "seq", 1)
        dy_across = lax.ppermute(after(slot_dy[0], across_far), "seq", MIDDLE)
        x_first = joined(first_near, [first_far])
        x_across = joined(across_near, [across_far])
        early = [
            jnp.where(place[0] == 0, array[:, half:], array[:, :half])
            for array in (slot_x[0], slot_dy[0])
        ]
        early = jnp.concatenate(early, axis=1)
        early = jnp.pad(early, ((0, tall - early.shape[0]), (0, 0)))
        early_far = send_xor(early, "dp", 2)
        x_relayed = lax.ppermute(after(x_first, x_across), "seq", MIDDLE)
        x_near = lax.ppermute(after(x_across, x_first), "seq", OUTWARD)
        dy_relayed = lax.ppermute(after(dy_first, dy_across), "seq", MIDDLE)
        dy_near = lax.ppermute(after(dy_across, dy_first), "seq", OUTWARD)
        parts, far, owns = work([[slot_x[0]], [x_first]], [[slot_dy[0]], [dy_first]], early_far)
        x_far = lax.ppermute(after(x_relayed, x_near, parts[0]), "seq", OUTWARD)
        dy_far = lax.ppermute(after(dy_relayed, dy_near), "seq", OUTWARD)
        home_far = [send_home(rows_of(parts[0], k), k, 0) for k in others]
        sums = weight_work(
            place,
            width,
            feat_width,
            [
                (owns[0], [whole(0)]),
                (owns[1], [whole(1)]),
                (early_far, [(2, 0, 0, feat_width)]),
                (far, [whole(3), (2, both, feat_width, wide)]),
            ],
            [],
        )
        parts_two, far_two, owns_two = work(
            [[x_near, x_relayed]],
            [[dy_near, dy_relayed]],
            far,
        )
        sent = after(parts_two[0], x_far, sums[0])
        over = lax.ppermute(sent, "seq", MIDDLE)
        into = lax.ppermute(sent, "seq", INWARD)
        parts_three, far_three, owns_three = work(
            [[after(x_far, far_two, *home_far), x_across]],
            [[dy_far, dy_across]],
            far_two,
        )
        onward = after(parts[1], parts_three[0]).astype(F32) + over.astype(F32)
        last = (parts_three[0].astype(F32) + into.astype(F32)).astype(BF)
        returned = [(onward.astype(BF), 1), (last, 3)]
        homes = [[rows_of(parts[0], 0)]] + [[array] for array in home_far]
        latest = [(owns_two, far_two), (owns_three, far_three)]
    else:
        sums, latest, returned, homes = [], [], [], [[] for _ in range(expert_count)]
        for j in range(seq_count):
            x_rows, dy_rows = [send_home(array, 0, j) for array in (slot_x[0], slot_dy[0])]
            parts, far, owns = work([[x_rows]], [[dy_rows]])
            returned.append((parts[0], j))
            latest.append((owns, far))
    for j in range(0, len(latest), 2):
        pair = latest[j : j + 2]
        arrays = [array for owns, far in pair for array in (owns[0], far)]
        sources = [(array, [whole(n)]) for n, array in enumerate(arrays)]
        sums = weight_work(place, width, feat_width, sources, sums)
    for k in range(expert_count):
        homes[k] += [send_home(rows_of(part, k), k, j) for part, j in returned]
        homes[k] = sum(part.astype(F32) for part in homes[k]).astype(BF)
    home_x = jnp.concatenate(homes, axis=0)

    keep_gu, keep_d, give_gu, give_d = sums
    gate_up = (keep_gu.astype(F32) + send_xor(give_gu, "dp", 1).astype(F32)).astype(BF)
    down_w_grad = (keep_d.astype(F32) + send_xor(give_d, "dp", 1).astype(F32)).astype(BF)
    gate_w_grad, up_w_grad = gate_up[:, :width], gate_up[:, width:]

    placer = placer_of(0, expert_count)
    placer = placer.astype(BF)
    token_grad = dot(placer, home_x[:, :feat_width], CONTRACT_FIRST).astype(BF)
    home_g = dot(placer, home_x[:, feat_width:], CONTRACT_FIRST)[:, 0]
    gate_grad = (home_g / prob).astype(BF)
    return (token_grad, gate_grad, gate_w_grad[None], up_w_grad[None], down_w_grad[None])


def solution(mesh):
    placed = (
        P(("dp", "expert", "seq"), None),
        P(("dp", "expert", "seq"), None),
        P(("dp", "expert", "seq")),
        P(("dp", "expert", "seq"), None),
        P("expert", None, "seq"),
        P("expert", None, "seq"),
        P("expert", "seq", None),
    )
    return jax.shard_map(
        body,
        mesh=mesh,
        in_specs=placed,
        out_specs=(
            P(("dp", "expert", "seq"), None),
            P(("dp", "expert", "seq")),
            P("expert", "dp", "seq"),
            P("expert", "dp", "seq"),
            P("expert", "seq", "dp"),
        ),
        check_vma=False,
    )
```

```python
import functools

import jax
import jax.numpy as jnp
from jax import lax
from jax.experimental import pallas as pl
from jax.experimental.pallas import tpu as pltpu
from jax.sharding import PartitionSpec as P

TOP = 1
BF = jnp.bfloat16
F32 = jnp.float32
PLAIN = (((1,), (0,)), ((), ()))
CONTRACT_LAST = (((1,), (1,)), ((), ()))
CONTRACT_FIRST = (((0,), (0,)), ((), ()))
MIDDLE = [(1, 2), (2, 1)]
OUTWARD = [(1, 0), (2, 3)]
INWARD = [(0, 1), (3, 2)]


def dot(left, right, dims=PLAIN):
    return lax.dot_general(left, right, dims, preferred_element_type=F32)


def after(value, *others):
    return lax.optimization_barrier((value,) + others)[0]


def send_xor(value, axis, mask):
    size = lax.axis_size(axis)
    return lax.ppermute(value, axis, [(i, i ^ mask) for i in range(size)])


def send_home(value, expert_mask, seq_mask):
    if not expert_mask:
        return send_xor(value, "seq", seq_mask) if seq_mask else value
    if not seq_mask:
        return send_xor(value, "expert", expert_mask)
    seq_count = lax.axis_size("seq")
    total = lax.axis_size("expert") * seq_count
    mask = expert_mask * seq_count + seq_mask
    return lax.ppermute(value, ("expert", "seq"), [(i, i ^ mask) for i in range(total)])


def slot_kernel(blocks, count, choices, place, *refs):
    xs, refs = refs[: count * choices], refs[count * choices :]
    dys, refs = refs[: count * choices], refs[count * choices :]
    wg, wu, wd, refs = refs[0], refs[1], refs[2], refs[3:]
    parts, refs = refs[:count], refs[count:]
    far_share, refs = refs[0], refs[1:]
    own_shares, refs = refs[:count], refs[count:]
    kx, ky, kg, ku, kd, kp, kfar, kown, sems, out_sems = refs
    feat, width = kg.shape
    rows = kx.shape[1]
    step = feat // blocks
    half = feat // 2
    low = 2 * half
    wide = kown.shape[2] - low

    def weights(i):
        cols = pl.ds(i * step, step)
        pairs = [(wg.at[cols], kg.at[cols]), (wu.at[cols], ku.at[cols])]
        return pairs + [(wd.at[:, cols], kd.at[:, cols])]

    def tokens(i, choice):
        cols = pl.ds(i * step, step)
        pairs = []
        for n in range(count):
            pairs += [(xs[n * choices + choice].at[:, cols], kx.at[n, :, cols])]
            pairs += [(dys[n * choices + choice].at[:, cols], ky.at[n, :, cols])]
        return pairs

    def copies_of(i, pairs, first):
        return [
            pltpu.make_async_copy(source, target, sems.at[first + k, i])
            for k, (source, target) in enumerate(pairs)
        ]

    def start_tokens(choice):
        for i in range(blocks):
            for copy in copies_of(i, tokens(i, choice), 3):
                copy.start()

    for i in range(blocks):
        for copy in copies_of(i, weights(i), 0):
            copy.start()
        if i == 0:
            if choices == 1:
                start_tokens(0)
            else:
                for choice in range(choices):
                    pl.when(place[2] == choice)(functools.partial(start_tokens, choice))
    copies = [copies_of(i, weights(i), 0) + copies_of(i, tokens(i, 0), 3) for i in range(blocks)]
    sums = [None] * count
    for i in range(blocks):
        for copy in copies[i]:
            copy.wait()
        cols = pl.ds(i * step, step)
        for n in range(count):
            terms = (
                dot(kx[n, :, cols], kg[cols]),
                dot(kx[n, :, cols], ku[cols]),
                dot(ky[n, :, cols], kd[:, cols], CONTRACT_LAST),
            )
            sums[n] = [s + t for s, t in zip(sums[n], terms)] if i else terms
    outs = []
    backward = []
    side = place[0]
    mine = pl.ds(pl.multiple_of(side * half, half), half)
    other = pl.ds(pl.multiple_of((1 - side) * half, half), half)
    if kfar.shape[0] > rows:
        kfar[rows:] = jnp.zeros((kfar.shape[0] - rows, kfar.shape[1]), BF)
    for n in range(count):
        gate_pre, up_pre, scaled_grad = sums[n]
        sigmoid_gate = jax.nn.sigmoid(gate_pre)
        activated = gate_pre * sigmoid_gate
        hidden = activated * up_pre
        gate_part = jnp.sum(hidden * scaled_grad, axis=1, keepdims=True).astype(BF)
        kp[n, :, feat:] = jnp.broadcast_to(gate_part, (rows, kp.shape[2] - feat))
        gate_delta = (
            scaled_grad * up_pre * sigmoid_gate * (1.0 + gate_pre * (1.0 - sigmoid_gate))
        ).astype(BF)
        up_delta = (scaled_grad * activated).astype(BF)
        backward.append((gate_delta, up_delta))
        kown[n, :rows, :half] = kx[n, :, mine]
        kown[n, :rows, half:low] = ky[n, :, mine]
        last = n == count - 1
        if last:
            kfar[:rows, :half] = kx[n, :, other]
            kfar[:rows, half:low] = ky[n, :, other]
        start = low if last else low + (n + 1) * wide
        for k, delta in enumerate((gate_delta, up_delta, hidden.astype(BF))):
            kown[n, :rows, low + k * width : low + (k + 1) * width] = delta
            kfar[:rows, start + k * width : start + (k + 1) * width] = delta
        if kown.shape[1] > rows:
            kown[n, rows:] = jnp.zeros((kown.shape[1] - rows, kown.shape[2]), BF)
        outs.append(pltpu.make_async_copy(kown.at[n], own_shares[n], out_sems.at[len(outs)]))
        outs[-1].start()
    outs.append(pltpu.make_async_copy(kfar, far_share, out_sems.at[len(outs)]))
    outs[-1].start()
    for i in range(blocks):
        cols = pl.ds(i * step, step)
        taken = pl.ds(i * step, kp.shape[2] - i * step) if i == blocks - 1 else cols
        for n, (gate_delta, up_delta) in enumerate(backward):
            kp[n, :, cols] = (
                dot(gate_delta, kg[cols], CONTRACT_LAST) + dot(up_delta, ku[cols], CONTRACT_LAST)
            ).astype(BF)
            outs.append(
                pltpu.make_async_copy(
                    kp.at[n, :, taken], parts[n].at[:, taken], out_sems.at[len(outs)]
                )
            )
            outs[-1].start()
    for copy in outs:
        copy.wait()


def slot_work(place, xs, dys, gate_local, up_local, down_local):
    rows, feat = xs[0][0].shape
    count, choices = len(xs), len(xs[0])
    width = gate_local.shape[1]
    tall = -(-rows // 16) * 16
    wide = -(-3 * width // 128) * 128
    blocks = 4
    away = pl.BlockSpec(memory_space=pltpu.HBM)
    far_shape, own_shape = (tall, feat + count * wide), (tall, feat + wide)
    outs = pl.pallas_call(
        functools.partial(slot_kernel, blocks, count, choices),
        out_shape=[jax.ShapeDtypeStruct((rows, feat + 128), BF)] * count
        + [jax.ShapeDtypeStruct(far_shape, BF)]
        + [jax.ShapeDtypeStruct(own_shape, BF)] * count,
        in_specs=[pl.BlockSpec(memory_space=pltpu.SMEM)] + [away] * (2 * count * choices + 3),
        out_specs=[away] * (2 * count + 1),
        scratch_shapes=[
            pltpu.VMEM((count, rows, feat), BF),
            pltpu.VMEM((count, rows, feat), BF),
            pltpu.VMEM((feat, width), BF),
            pltpu.VMEM((feat, width), BF),
            pltpu.VMEM((width, feat), BF),
            pltpu.VMEM((count, rows, feat + 128), BF),
            pltpu.VMEM(far_shape, BF),
            pltpu.VMEM((count,) + own_shape, BF),
            pltpu.SemaphoreType.DMA((3 + 2 * count, blocks)),
            pltpu.SemaphoreType.DMA((1 + count + count * blocks,)),
        ],
        compiler_params=pltpu.CompilerParams(vmem_limit_bytes=32 * 1024 * 1024),
        name="slot_work",
    )(place, *sum(xs, []), *sum(dys, []), gate_local, up_local, down_local)
    return outs[:count], outs[count], outs[count + 1 :]


def weight_kernel(cuts, started, width, place, *refs):
    arrays, refs = refs[: len(cuts)], refs[len(cuts) :]
    before, refs = (refs[:4], refs[4:]) if started else ([], refs)
    outs, refs = refs[:4], refs[4:]
    rows, sums_gu, sums_d, old_gu, old_d, sems, old_sems = refs
    quarter = sums_gu.shape[1]
    half = 2 * quarter
    low = 2 * half
    mine = place[1]
    tall = arrays[0].shape[0]
    copies = []
    for array, pieces in zip(arrays, cuts):
        for block, start, target, size in pieces:
            copies.append(
                pltpu.make_async_copy(
                    array.at[:, pl.ds(start, size)],
                    rows.at[pl.ds(block * tall, tall), pl.ds(target, size)],
                    sems.at[len(copies)],
                )
            )
    places = [(mine, 0), (mine, 1), (1 - mine, 0), (1 - mine, 1)]
    for k, ref in enumerate(before):
        side, kind = places[k]
        copies.append(
            pltpu.make_async_copy(ref, (old_gu, old_d)[kind].at[side], old_sems.at[k])
        )
    for copy in copies:
        copy.start()
    for copy in copies:
        copy.wait()
    cut = quarter // 2
    for q in range(2):
        for c in range(2):
            x_cols = pl.ds(q * quarter + c * cut, cut)
            dy_cols = pl.ds(half + q * quarter + c * cut, cut)
            cols = pl.ds(c * cut, cut)
            gate_up = dot(rows[:, x_cols], rows[:, low : low + 2 * width], CONTRACT_FIRST)
            hidden = rows[:, low + 2 * width : low + 3 * width]
            down = dot(hidden, rows[:, dy_cols], CONTRACT_FIRST)
            if started:
                gate_up += old_gu[q, cols].astype(F32)
                down += old_d[q, :, cols].astype(F32)
            sums_gu[q, cols] = gate_up.astype(BF)
            sums_d[q, :, cols] = down.astype(BF)
    copies = [
        pltpu.make_async_copy((sums_gu, sums_d)[kind].at[side], outs[k], old_sems.at[k])
        for k, (side, kind) in enumerate(places)
    ]
    for copy in copies:
        copy.start()
    for copy in copies:
        copy.wait()


def weight_work(place, width, feat, sources, before):
    tall = sources[0][0].shape[0]
    wide = -(-3 * width // 128) * 128
    quarter = feat // 4
    arrays = [array for array, _ in sources]
    cuts = [pieces for _, pieces in sources]
    count = 1 + max(piece[0] for pieces in cuts for piece in pieces)
    away = pl.BlockSpec(memory_space=pltpu.HBM)
    shapes = [(quarter, 2 * width), (width, quarter)] * 2
    kept = [(2,) + shape for shape in shapes[:2]]
    return pl.pallas_call(
        functools.partial(weight_kernel, cuts, bool(before), width),
        out_shape=[jax.ShapeDtypeStruct(shape, BF) for shape in shapes],
        in_specs=[pl.BlockSpec(memory_space=pltpu.SMEM)]
        + [away] * (len(arrays) + len(before)),
        out_specs=[away] * 4,
        scratch_shapes=[pltpu.VMEM((count * tall, feat + wide), BF)]
        + [pltpu.VMEM(shape, BF) for shape in kept * 2]
        + [
            pltpu.SemaphoreType.DMA((sum(len(pieces) for pieces in cuts),)),
            pltpu.SemaphoreType.DMA((4,)),
        ],
        compiler_params=pltpu.CompilerParams(vmem_limit_bytes=32 * 1024 * 1024),
        name="weight_work",
    )(place, *arrays, *before)


def final_kernel(keep_gu, keep_d, came_gu, came_d, gate, up, down):
    width = gate.shape[1]
    gate_up = keep_gu[...].astype(F32) + came_gu[...].astype(F32)
    gate[...] = gate_up[:, :width].astype(BF)
    up[...] = gate_up[:, width:].astype(BF)
    down[...] = (keep_d[...].astype(F32) + came_d[...].astype(F32)).astype(BF)


def final_sums(keep_gu, keep_d, came_gu, came_d):
    quarter, width = keep_d.shape[1], keep_d.shape[0]
    steps = 4
    high = quarter // steps
    tall = [pl.BlockSpec((high, 2 * width), lambda i: (i, 0))]
    wide = [pl.BlockSpec((width, high), lambda i: (0, i))]
    thin = [pl.BlockSpec((high, width), lambda i: (i, 0))]
    shapes = [(quarter, width), (quarter, width), (width, quarter)]
    return pl.pallas_call(
        final_kernel,
        grid=(steps,),
        out_shape=[jax.ShapeDtypeStruct(shape, BF) for shape in shapes],
        in_specs=(tall + wide) * 2,
        out_specs=thin * 2 + wide,
        compiler_params=pltpu.CompilerParams(vmem_limit_bytes=32 * 1024 * 1024),
        name="final_sums",
    )(keep_gu, keep_d, came_gu, came_d)


def body(tokens, out_grad, gate_prob, expert_ids, w_gate, w_up, w_down):
    expert_count = lax.axis_size("expert")
    seq_count = lax.axis_size("seq")
    tok_rows, feat_width = tokens.shape
    capacity = tok_rows * TOP * 17 // (16 * expert_count)
    my_expert = lax.axis_index("expert")
    my_seq = lax.axis_index("seq")
    route = expert_ids[:, 0]
    onehot = (route[:, None] == jnp.arange(expert_count)[None, :]).astype(F32)
    earlier = (jnp.arange(tok_rows)[:, None] > jnp.arange(tok_rows)[None, :]).astype(F32)
    before = dot(earlier, onehot)
    slot_index = jnp.sum(before * onehot, axis=1).astype(jnp.int32)
    block = jnp.bitwise_xor(route, my_expert)
    target = block * capacity + slot_index
    prob = gate_prob.astype(F32)

    def placer_of(first, last):
        rows = first * capacity + jnp.arange((last - first) * capacity)
        return rows[:, None] == target[None, :]

    def pack_x(first, last):
        return dot(placer_of(first, last).astype(BF), tokens).astype(BF)

    def pack_dy(first, last):
        scaler = jnp.where(placer_of(first, last), prob[None, :], 0.0).astype(BF)
        return dot(scaler, out_grad).astype(BF)

    def joined(first, rest):
        return jnp.concatenate([first] + list(rest), axis=0)

    gate_local, up_local, down_local = w_gate[0], w_up[0], w_down[0]
    others = range(1, expert_count)
    far_x = [pack_x(j, j + 1) for j in others]
    near_x = after(pack_x(0, 1), *far_x)
    out_grad = after(out_grad, near_x)
    far_x = [send_xor(far_x[j - 1], "expert", j) for j in others]
    far_dy = [send_xor(after(pack_dy(j, j + 1), *far_x), "expert", j) for j in others]
    near_dy = pack_dy(0, 1)
    far_x = far_x[0] if len(far_x) == 1 else jnp.concatenate(far_x, axis=0)
    slot_x = [joined(near_x, [far_x])]
    slot_dy = [joined(near_dy, far_dy)]

    dp_index = lax.axis_index("dp")
    is_inner = (my_seq > 0) & (my_seq < seq_count - 1)
    place = jnp.stack([dp_index // 2, dp_index % 2, is_inner]).astype(jnp.int32)
    width = gate_local.shape[1]
    wide = -(-3 * width // 128) * 128
    both = feat_width + wide
    half = feat_width // 2
    tall = -(-expert_count * capacity // 16) * 16

    def work(xs, dys, *others):
        parts, far_share, own_shares = slot_work(
            place, xs, dys, gate_local, up_local, down_local
        )
        far = send_xor(after(far_share, *others), "dp", 2)
        return parts, far, own_shares

    def whole(block):
        return (block, 0, 0, both)

    def rows_of(array, k):
        return array[k * capacity : (k + 1) * capacity]

    if seq_count == 4:
        first_near = send_xor(near_x, "seq", 1)
        across_near = lax.ppermute(near_x, "seq", MIDDLE)
        first_far = send_xor(far_x, "seq", 1)
        across_far = lax.ppermute(far_x, "seq", MIDDLE)
        dy_first = send_xor(slot_dy[0], "seq", 1)
        dy_across = lax.ppermute(after(slot_dy[0], across_far), "seq", MIDDLE)
        x_first = joined(first_near, [first_far])
        x_across = joined(across_near, [across_far])
        early = [
            jnp.where(place[0] == 0, array[:, half:], array[:, :half])
            for array in (slot_x[0], slot_dy[0])
        ]
        early = jnp.concatenate(early, axis=1)
        early = jnp.pad(early, ((0, tall - early.shape[0]), (0, 0)))
        early_far = send_xor(early, "dp", 2)
        x_relayed = lax.ppermute(after(x_first, x_across), "seq", MIDDLE)
        x_near = lax.ppermute(after(x_across, x_first), "seq", OUTWARD)
        dy_relayed = lax.ppermute(after(dy_first, dy_across), "seq", MIDDLE)
        dy_near = lax.ppermute(after(dy_across, dy_first), "seq", OUTWARD)
        parts, far, owns = work([[slot_x[0]], [x_first]], [[slot_dy[0]], [dy_first]], early_far)
        x_far = lax.ppermute(after(x_relayed, x_near, parts[0]), "seq", OUTWARD)
        dy_far = lax.ppermute(after(dy_relayed, dy_near), "seq", OUTWARD)
        home_far = [send_home(rows_of(parts[0], k), k, 0) for k in others]
        sums = weight_work(
            place,
            width,
            feat_width,
            [
                (owns[0], [whole(0)]),
                (owns[1], [whole(1)]),
                (early_far, [(2, 0, 0, feat_width)]),
                (far, [whole(3), (2, both, feat_width, wide)]),
            ],
            [],
        )
        parts_two, far_two, owns_two = work(
            [[x_near, x_relayed]],
            [[dy_near, dy_relayed]],
            far,
        )
        sent = after(parts_two[0], x_far, sums[0])
        over = lax.ppermute(sent, "seq", MIDDLE)
        into = lax.ppermute(sent, "seq", INWARD)
        parts_three, far_three, owns_three = work(
            [[after(x_far, far_two, *home_far), x_across]],
            [[dy_far, dy_across]],
            far_two,
        )
        onward = after(parts[1], parts_three[0]).astype(F32) + over.astype(F32)
        last = (parts_three[0].astype(F32) + into.astype(F32)).astype(BF)
        returned = [(onward.astype(BF), 1), (last, 3)]
        homes = [[rows_of(parts[0], 0)]] + [[array] for array in home_far]
        latest = [(owns_two, far_two), (owns_three, far_three)]
    else:
        sums, latest, returned, homes = [], [], [], [[] for _ in range(expert_count)]
        for j in range(seq_count):
            x_rows, dy_rows = [send_home(array, 0, j) for array in (slot_x[0], slot_dy[0])]
            parts, far, owns = work([[x_rows]], [[dy_rows]])
            returned.append((parts[0], j))
            latest.append((owns, far))
    for j in range(0, len(latest), 2):
        pair = latest[j : j + 2]
        arrays = [array for owns, far in pair for array in (owns[0], far)]
        sources = [(array, [whole(n)]) for n, array in enumerate(arrays)]
        sums = weight_work(place, width, feat_width, sources, sums)
    for k in range(expert_count):
        homes[k] += [send_home(rows_of(part, k), k, j) for part, j in returned]
        homes[k] = sum(part.astype(F32) for part in homes[k]).astype(BF)
    home_x = jnp.concatenate(homes, axis=0)

    keep_gu, keep_d, give_gu, give_d = sums
    gate_w_grad, up_w_grad, down_w_grad = final_sums(
        keep_gu, keep_d, send_xor(give_gu, "dp", 1), send_xor(give_d, "dp", 1)
    )

    placer = placer_of(0, expert_count)
    placer = placer.astype(BF)
    token_grad = dot(placer, home_x[:, :feat_width], CONTRACT_FIRST).astype(BF)
    home_g = dot(placer, home_x[:, feat_width:], CONTRACT_FIRST)[:, 0]
    gate_grad = (home_g / prob).astype(BF)
    return (token_grad, gate_grad, gate_w_grad[None], up_w_grad[None], down_w_grad[None])


def solution(mesh):
    placed = (
        P(("dp", "expert", "seq"), None),
        P(("dp", "expert", "seq"), None),
        P(("dp", "expert", "seq")),
        P(("dp", "expert", "seq"), None),
        P("expert", None, "seq"),
        P("expert", None, "seq"),
        P("expert", "seq", None),
    )
    return jax.shard_map(
        body,
        mesh=mesh,
        in_specs=placed,
        out_specs=(
            P(("dp", "expert", "seq"), None),
            P(("dp", "expert", "seq")),
            P("expert", "dp", "seq"),
            P("expert", "dp", "seq"),
            P("expert", "seq", "dp"),
        ),
        check_vma=False,
    )
```

```python
import functools

import jax
import jax.numpy as jnp
from jax import lax
from jax.experimental import pallas as pl
from jax.experimental.pallas import tpu as pltpu
from jax.sharding import PartitionSpec as P

TOP = 1
BF = jnp.bfloat16
F32 = jnp.float32
PLAIN = (((1,), (0,)), ((), ()))
CONTRACT_LAST = (((1,), (1,)), ((), ()))
CONTRACT_FIRST = (((0,), (0,)), ((), ()))
MIDDLE = [(1, 2), (2, 1)]
OUTWARD = [(1, 0), (2, 3)]
INWARD = [(0, 1), (3, 2)]


def dot(left, right, dims=PLAIN):
    return lax.dot_general(left, right, dims, preferred_element_type=F32)


def after(value, *others):
    return lax.optimization_barrier((value,) + others)[0]


def send_xor(value, axis, mask):
    size = lax.axis_size(axis)
    return lax.ppermute(value, axis, [(i, i ^ mask) for i in range(size)])


def send_home(value, expert_mask, seq_mask):
    if not expert_mask:
        return send_xor(value, "seq", seq_mask) if seq_mask else value
    if not seq_mask:
        return send_xor(value, "expert", expert_mask)
    seq_count = lax.axis_size("seq")
    total = lax.axis_size("expert") * seq_count
    mask = expert_mask * seq_count + seq_mask
    return lax.ppermute(value, ("expert", "seq"), [(i, i ^ mask) for i in range(total)])


def slot_kernel(blocks, count, choices, place, *refs):
    xs, refs = refs[: count * choices], refs[count * choices :]
    dys, refs = refs[: count * choices], refs[count * choices :]
    wg, wu, wd, refs = refs[0], refs[1], refs[2], refs[3:]
    parts, refs = refs[:count], refs[count:]
    far_share, refs = refs[0], refs[1:]
    own_shares, refs = refs[:count], refs[count:]
    kx, ky, kg, ku, kd, kp, kfar, kown, sems, out_sems = refs
    feat, width = kg.shape
    rows = kx.shape[1]
    step = feat // blocks
    half = feat // 2
    low = 2 * half
    wide = kown.shape[2] - low

    def weights(i):
        cols = pl.ds(i * step, step)
        pairs = [(wg.at[cols], kg.at[cols]), (wu.at[cols], ku.at[cols])]
        return pairs + [(wd.at[:, cols], kd.at[:, cols])]

    def tokens(i, choice):
        cols = pl.ds(i * step, step)
        pairs = []
        for n in range(count):
            pairs += [(xs[n * choices + choice].at[:, cols], kx.at[n, :, cols])]
            pairs += [(dys[n * choices + choice].at[:, cols], ky.at[n, :, cols])]
        return pairs

    def copies_of(i, pairs, first):
        return [
            pltpu.make_async_copy(source, target, sems.at[first + k, i])
            for k, (source, target) in enumerate(pairs)
        ]

    def start_tokens(choice):
        for i in range(blocks):
            for copy in copies_of(i, tokens(i, choice), 3):
                copy.start()

    for i in range(blocks):
        for copy in copies_of(i, weights(i), 0):
            copy.start()
        if i == 0:
            if choices == 1:
                start_tokens(0)
            else:
                for choice in range(choices):
                    pl.when(place[2] == choice)(functools.partial(start_tokens, choice))
    copies = [copies_of(i, weights(i), 0) + copies_of(i, tokens(i, 0), 3) for i in range(blocks)]
    sums = [None] * count
    for i in range(blocks):
        for copy in copies[i]:
            copy.wait()
        cols = pl.ds(i * step, step)
        for n in range(count):
            terms = (
                dot(kx[n, :, cols], kg[cols]),
                dot(kx[n, :, cols], ku[cols]),
                dot(ky[n, :, cols], kd[:, cols], CONTRACT_LAST),
            )
            sums[n] = [s + t for s, t in zip(sums[n], terms)] if i else terms
    outs = []
    backward = []
    side = place[0]
    mine = pl.ds(pl.multiple_of(side * half, half), half)
    other = pl.ds(pl.multiple_of((1 - side) * half, half), half)
    if kfar.shape[0] > rows:
        kfar[rows:] = jnp.zeros((kfar.shape[0] - rows, kfar.shape[1]), BF)
    for n in range(count):
        gate_pre, up_pre, scaled_grad = sums[n]
        sigmoid_gate = jax.nn.sigmoid(gate_pre)
        activated = gate_pre * sigmoid_gate
        hidden = activated * up_pre
        gate_part = jnp.sum(hidden * scaled_grad, axis=1, keepdims=True).astype(BF)
        kp[n, :, feat:] = jnp.broadcast_to(gate_part, (rows, kp.shape[2] - feat))
        gate_delta = (
            scaled_grad * up_pre * sigmoid_gate * (1.0 + gate_pre * (1.0 - sigmoid_gate))
        ).astype(BF)
        up_delta = (scaled_grad * activated).astype(BF)
        backward.append((gate_delta, up_delta))
        kown[n, :rows, :half] = kx[n, :, mine]
        kown[n, :rows, half:low] = ky[n, :, mine]
        last = n == count - 1
        if last:
            kfar[:rows, :half] = kx[n, :, other]
            kfar[:rows, half:low] = ky[n, :, other]
        start = low if last else low + (n + 1) * wide
        for k, delta in enumerate((gate_delta, up_delta, hidden.astype(BF))):
            kown[n, :rows, low + k * width : low + (k + 1) * width] = delta
            kfar[:rows, start + k * width : start + (k + 1) * width] = delta
        if kown.shape[1] > rows:
            kown[n, rows:] = jnp.zeros((kown.shape[1] - rows, kown.shape[2]), BF)
        outs.append(pltpu.make_async_copy(kown.at[n], own_shares[n], out_sems.at[len(outs)]))
        outs[-1].start()
    outs.append(pltpu.make_async_copy(kfar, far_share, out_sems.at[len(outs)]))
    outs[-1].start()
    for i in range(blocks):
        cols = pl.ds(i * step, step)
        taken = pl.ds(i * step, kp.shape[2] - i * step) if i == blocks - 1 else cols
        for n, (gate_delta, up_delta) in enumerate(backward):
            kp[n, :, cols] = (
                dot(gate_delta, kg[cols], CONTRACT_LAST) + dot(up_delta, ku[cols], CONTRACT_LAST)
            ).astype(BF)
            outs.append(
                pltpu.make_async_copy(
                    kp.at[n, :, taken], parts[n].at[:, taken], out_sems.at[len(outs)]
                )
            )
            outs[-1].start()
    for copy in outs:
        copy.wait()


def slot_work(place, xs, dys, gate_local, up_local, down_local):
    rows, feat = xs[0][0].shape
    count, choices = len(xs), len(xs[0])
    width = gate_local.shape[1]
    tall = -(-rows // 16) * 16
    wide = -(-3 * width // 128) * 128
    blocks = 4
    away = pl.BlockSpec(memory_space=pltpu.HBM)
    far_shape, own_shape = (tall, feat + count * wide), (tall, feat + wide)
    outs = pl.pallas_call(
        functools.partial(slot_kernel, blocks, count, choices),
        out_shape=[jax.ShapeDtypeStruct((rows, feat + 128), BF)] * count
        + [jax.ShapeDtypeStruct(far_shape, BF)]
        + [jax.ShapeDtypeStruct(own_shape, BF)] * count,
        in_specs=[pl.BlockSpec(memory_space=pltpu.SMEM)] + [away] * (2 * count * choices + 3),
        out_specs=[away] * (2 * count + 1),
        scratch_shapes=[
            pltpu.VMEM((count, rows, feat), BF),
            pltpu.VMEM((count, rows, feat), BF),
            pltpu.VMEM((feat, width), BF),
            pltpu.VMEM((feat, width), BF),
            pltpu.VMEM((width, feat), BF),
            pltpu.VMEM((count, rows, feat + 128), BF),
            pltpu.VMEM(far_shape, BF),
            pltpu.VMEM((count,) + own_shape, BF),
            pltpu.SemaphoreType.DMA((3 + 2 * count, blocks)),
            pltpu.SemaphoreType.DMA((1 + count + count * blocks,)),
        ],
        compiler_params=pltpu.CompilerParams(vmem_limit_bytes=28 * 1024 * 1024),
        name="slot_work",
    )(place, *sum(xs, []), *sum(dys, []), gate_local, up_local, down_local)
    return outs[:count], outs[count], outs[count + 1 :]


def weight_kernel(cuts, started, width, place, *refs):
    arrays, refs = refs[: len(cuts)], refs[len(cuts) :]
    before, refs = (refs[:4], refs[4:]) if started else ([], refs)
    outs, refs = refs[:4], refs[4:]
    rows, sums_gu, sums_d, old_gu, old_d, sems, old_sems = refs
    quarter = sums_gu.shape[1]
    half = 2 * quarter
    low = 2 * half
    mine = place[1]
    tall = arrays[0].shape[0]
    copies = []
    for array, pieces in zip(arrays, cuts):
        for block, start, target, size in pieces:
            copies.append(
                pltpu.make_async_copy(
                    array.at[:, pl.ds(start, size)],
                    rows.at[pl.ds(block * tall, tall), pl.ds(target, size)],
                    sems.at[len(copies)],
                )
            )
    places = [(mine, 0), (mine, 1), (1 - mine, 0), (1 - mine, 1)]
    for k, ref in enumerate(before):
        side, kind = places[k]
        copies.append(
            pltpu.make_async_copy(ref, (old_gu, old_d)[kind].at[side], old_sems.at[k])
        )
    for copy in copies:
        copy.start()
    for copy in copies:
        copy.wait()
    cut = quarter // 2
    for q in range(2):
        for c in range(2):
            x_cols = pl.ds(q * quarter + c * cut, cut)
            dy_cols = pl.ds(half + q * quarter + c * cut, cut)
            cols = pl.ds(c * cut, cut)
            gate_up = dot(rows[:, x_cols], rows[:, low : low + 2 * width], CONTRACT_FIRST)
            hidden = rows[:, low + 2 * width : low + 3 * width]
            down = dot(hidden, rows[:, dy_cols], CONTRACT_FIRST)
            if started:
                gate_up += old_gu[q, cols].astype(F32)
                down += old_d[q, :, cols].astype(F32)
            sums_gu[q, cols] = gate_up.astype(BF)
            sums_d[q, :, cols] = down.astype(BF)
    copies = [
        pltpu.make_async_copy((sums_gu, sums_d)[kind].at[side], outs[k], old_sems.at[k])
        for k, (side, kind) in enumerate(places)
    ]
    for copy in copies:
        copy.start()
    for copy in copies:
        copy.wait()


def weight_work(place, width, feat, sources, before):
    tall = sources[0][0].shape[0]
    wide = -(-3 * width // 128) * 128
    quarter = feat // 4
    arrays = [array for array, _ in sources]
    cuts = [pieces for _, pieces in sources]
    count = 1 + max(piece[0] for pieces in cuts for piece in pieces)
    away = pl.BlockSpec(memory_space=pltpu.HBM)
    shapes = [(quarter, 2 * width), (width, quarter)] * 2
    kept = [(2,) + shape for shape in shapes[:2]]
    return pl.pallas_call(
        functools.partial(weight_kernel, cuts, bool(before), width),
        out_shape=[jax.ShapeDtypeStruct(shape, BF) for shape in shapes],
        in_specs=[pl.BlockSpec(memory_space=pltpu.SMEM)]
        + [away] * (len(arrays) + len(before)),
        out_specs=[away] * 4,
        scratch_shapes=[pltpu.VMEM((count * tall, feat + wide), BF)]
        + [pltpu.VMEM(shape, BF) for shape in kept * 2]
        + [
            pltpu.SemaphoreType.DMA((sum(len(pieces) for pieces in cuts),)),
            pltpu.SemaphoreType.DMA((4,)),
        ],
        compiler_params=pltpu.CompilerParams(vmem_limit_bytes=28 * 1024 * 1024),
        name="weight_work",
    )(place, *arrays, *before)


def final_kernel(keep_gu, keep_d, came_gu, came_d, gate, up, down):
    width = gate.shape[1]
    gate_up = keep_gu[...].astype(F32) + came_gu[...].astype(F32)
    gate[...] = gate_up[:, :width].astype(BF)
    up[...] = gate_up[:, width:].astype(BF)
    down[...] = (keep_d[...].astype(F32) + came_d[...].astype(F32)).astype(BF)


def final_sums(keep_gu, keep_d, came_gu, came_d):
    quarter, width = keep_d.shape[1], keep_d.shape[0]
    steps = 4
    high = quarter // steps
    tall = [pl.BlockSpec((high, 2 * width), lambda i: (i, 0))]
    wide = [pl.BlockSpec((width, high), lambda i: (0, i))]
    thin = [pl.BlockSpec((high, width), lambda i: (i, 0))]
    shapes = [(quarter, width), (quarter, width), (width, quarter)]
    return pl.pallas_call(
        final_kernel,
        grid=(steps,),
        out_shape=[jax.ShapeDtypeStruct(shape, BF) for shape in shapes],
        in_specs=(tall + wide) * 2,
        out_specs=thin * 2 + wide,
        compiler_params=pltpu.CompilerParams(vmem_limit_bytes=28 * 1024 * 1024),
        name="final_sums",
    )(keep_gu, keep_d, came_gu, came_d)


def body(tokens, out_grad, gate_prob, expert_ids, w_gate, w_up, w_down):
    expert_count = lax.axis_size("expert")
    seq_count = lax.axis_size("seq")
    tok_rows, feat_width = tokens.shape
    capacity = tok_rows * TOP * 17 // (16 * expert_count)
    my_expert = lax.axis_index("expert")
    my_seq = lax.axis_index("seq")
    route = expert_ids[:, 0]
    onehot = (route[:, None] == jnp.arange(expert_count)[None, :]).astype(F32)
    earlier = (jnp.arange(tok_rows)[:, None] > jnp.arange(tok_rows)[None, :]).astype(F32)
    before = dot(earlier, onehot)
    slot_index = jnp.sum(before * onehot, axis=1).astype(jnp.int32)
    block = jnp.bitwise_xor(route, my_expert)
    target = block * capacity + slot_index
    prob = gate_prob.astype(F32)

    def placer_of(first, last):
        rows = first * capacity + jnp.arange((last - first) * capacity)
        return rows[:, None] == target[None, :]

    def pack_x(first, last):
        return dot(placer_of(first, last).astype(BF), tokens).astype(BF)

    def pack_dy(first, last):
        scaler = jnp.where(placer_of(first, last), prob[None, :], 0.0).astype(BF)
        return dot(scaler, out_grad).astype(BF)

    def joined(first, rest):
        return jnp.concatenate([first] + list(rest), axis=0)

    gate_local, up_local, down_local = w_gate[0], w_up[0], w_down[0]
    others = range(1, expert_count)
    far_x = [pack_x(j, j + 1) for j in others]
    near_x = after(pack_x(0, 1), *far_x)
    out_grad = after(out_grad, near_x)
    far_x = [send_xor(far_x[j - 1], "expert", j) for j in others]
    far_dy = [send_xor(after(pack_dy(j, j + 1), *far_x), "expert", j) for j in others]
    near_dy = pack_dy(0, 1)
    far_x = far_x[0] if len(far_x) == 1 else jnp.concatenate(far_x, axis=0)
    slot_x = [joined(near_x, [far_x])]
    slot_dy = [joined(near_dy, far_dy)]

    dp_index = lax.axis_index("dp")
    is_inner = (my_seq > 0) & (my_seq < seq_count - 1)
    place = jnp.stack([dp_index // 2, dp_index % 2, is_inner]).astype(jnp.int32)
    width = gate_local.shape[1]
    wide = -(-3 * width // 128) * 128
    both = feat_width + wide
    half = feat_width // 2
    tall = -(-expert_count * capacity // 16) * 16

    def work(xs, dys, *others):
        parts, far_share, own_shares = slot_work(
            place, xs, dys, gate_local, up_local, down_local
        )
        far = send_xor(after(far_share, *others), "dp", 2)
        return parts, far, own_shares

    def whole(block):
        return (block, 0, 0, both)

    def rows_of(array, k):
        return array[k * capacity : (k + 1) * capacity]

    if seq_count == 4:
        first_near = send_xor(near_x, "seq", 1)
        across_near = lax.ppermute(near_x, "seq", MIDDLE)
        first_far = send_xor(far_x, "seq", 1)
        across_far = lax.ppermute(far_x, "seq", MIDDLE)
        dy_first = send_xor(slot_dy[0], "seq", 1)
        dy_across = lax.ppermute(after(slot_dy[0], across_far), "seq", MIDDLE)
        x_first = joined(first_near, [first_far])
        x_across = joined(across_near, [across_far])
        early = [
            jnp.where(place[0] == 0, array[:, half:], array[:, :half])
            for array in (slot_x[0], slot_dy[0])
        ]
        early = jnp.concatenate(early, axis=1)
        early = jnp.pad(early, ((0, tall - early.shape[0]), (0, 0)))
        early_far = send_xor(early, "dp", 2)
        x_relayed = lax.ppermute(after(x_first, x_across), "seq", MIDDLE)
        x_near = lax.ppermute(after(x_across, x_first), "seq", OUTWARD)
        dy_relayed = lax.ppermute(after(dy_first, dy_across), "seq", MIDDLE)
        dy_near = lax.ppermute(after(dy_across, dy_first), "seq", OUTWARD)
        parts, far, owns = work([[slot_x[0]], [x_first]], [[slot_dy[0]], [dy_first]], early_far)
        x_far = lax.ppermute(after(x_relayed, x_near, parts[0]), "seq", OUTWARD)
        dy_far = lax.ppermute(after(dy_relayed, dy_near), "seq", OUTWARD)
        home_far = [send_home(rows_of(parts[0], k), k, 0) for k in others]
        sums = weight_work(
            place,
            width,
            feat_width,
            [
                (owns[0], [whole(0)]),
                (owns[1], [whole(1)]),
                (early_far, [(2, 0, 0, feat_width)]),
                (far, [whole(3), (2, both, feat_width, wide)]),
            ],
            [],
        )
        parts_two, far_two, owns_two = work(
            [[x_near, x_relayed]],
            [[dy_near, dy_relayed]],
            far,
        )
        sent = after(parts_two[0], x_far, sums[0])
        over = lax.ppermute(sent, "seq", MIDDLE)
        into = lax.ppermute(sent, "seq", INWARD)
        parts_three, far_three, owns_three = work(
            [[after(x_far, far_two, *home_far), x_across]],
            [[dy_far, dy_across]],
            far_two,
        )
        onward = after(parts[1], parts_three[0]).astype(F32) + over.astype(F32)
        last = (parts_three[0].astype(F32) + into.astype(F32)).astype(BF)
        returned = [(onward.astype(BF), 1), (last, 3)]
        homes = [[rows_of(parts[0], 0)]] + [[array] for array in home_far]
        latest = [(owns_two, far_two), (owns_three, far_three)]
    else:
        sums, latest, returned, homes = [], [], [], [[] for _ in range(expert_count)]
        for j in range(seq_count):
            x_rows, dy_rows = [send_home(array, 0, j) for array in (slot_x[0], slot_dy[0])]
            parts, far, owns = work([[x_rows]], [[dy_rows]])
            returned.append((parts[0], j))
            latest.append((owns, far))
    for j in range(0, len(latest), 2):
        pair = latest[j : j + 2]
        arrays = [array for owns, far in pair for array in (owns[0], far)]
        sources = [(array, [whole(n)]) for n, array in enumerate(arrays)]
        sums = weight_work(place, width, feat_width, sources, sums)
    for k in range(expert_count):
        homes[k] += [send_home(rows_of(part, k), k, j) for part, j in returned]
        homes[k] = sum(part.astype(F32) for part in homes[k]).astype(BF)
    home_x = jnp.concatenate(homes, axis=0)

    keep_gu, keep_d, give_gu, give_d = sums
    gate_w_grad, up_w_grad, down_w_grad = final_sums(
        keep_gu, keep_d, send_xor(give_gu, "dp", 1), send_xor(give_d, "dp", 1)
    )

    placer = placer_of(0, expert_count)
    placer = placer.astype(BF)
    token_grad = dot(placer, home_x[:, :feat_width], CONTRACT_FIRST).astype(BF)
    home_g = dot(placer, home_x[:, feat_width:], CONTRACT_FIRST)[:, 0]
    gate_grad = (home_g / prob).astype(BF)
    return (token_grad, gate_grad, gate_w_grad[None], up_w_grad[None], down_w_grad[None])


def solution(mesh):
    placed = (
        P(("dp", "expert", "seq"), None),
        P(("dp", "expert", "seq"), None),
        P(("dp", "expert", "seq")),
        P(("dp", "expert", "seq"), None),
        P("expert", None, "seq"),
        P("expert", None, "seq"),
        P("expert", "seq", None),
    )
    return jax.shard_map(
        body,
        mesh=mesh,
        in_specs=placed,
        out_specs=(
            P(("dp", "expert", "seq"), None),
            P(("dp", "expert", "seq")),
            P("expert", "dp", "seq"),
            P("expert", "dp", "seq"),
            P("expert", "seq", "dp"),
        ),
        check_vma=False,
    )
```
